32 devices in a mesh: wide: 8 (over z, y), narrow: 4 (over x, core).
Axes of the slice: x: 2, y: 2, z: 4, core: 2. Of those that a mesh axis runs over, the one named last changes fastest.
Arguments:
- slab: float32 [4, 512, 128, 256], P(None, 'narrow', 'wide'), may hold values from -180 to 180
- factor: float32 [512, 64], replicated, may hold values from -0.25 to 0.25
Outputs:
- r_factor: float32 [512, 512], replicated
- core: float32 [4, 64, 128, 256], P(None, None, 'wide', 'narrow')
The draws below stay inside these ranges and needn't reach their ends.
All inputs are finite; a program needn't handle non-finite values.
Results may differ from the reference program's by a relative error of at most 0.00007.
Values sent between devices are 32-bit elements; how exact they have to be, the bound alone decides.
A program may use at most 256 MiB of HBM per device.

```python
import math
import jax
import jax.numpy as jnp
from jax import lax

D1 = 512
RANK = 64
COMP = 4
I3 = 256
I2 = 128
NCOL = 131072


def draw_slab(key, part):
    keys = jax.random.split(key, 5)
    shape = (COMP, D1, I2, I3)
    noise = jnp.clip(jax.random.normal(keys[0], shape, jnp.float32), -6.0, 6.0)
    before = jnp.roll(noise, 1, axis=1)
    lean = jax.random.uniform(keys[1], (1, D1, 1, 1), jnp.float32, 0.3, 0.8)
    scale = jnp.exp(jax.random.uniform(keys[2], (1, D1, 1, 1), jnp.float32, math.log(0.5), math.log(5.0)))
    share = jax.random.uniform(keys[3], (1, D1, 1, 1), jnp.float32, -1.0, 1.0)
    rise = 1.0 + 2.0 * jnp.arange(I2, dtype=jnp.float32).reshape(1, 1, I2, 1) / max(I2 - 1, 1)
    common = jnp.clip(jax.random.normal(keys[4], (COMP, 1, I2, I3), jnp.float32), -6.0, 6.0)
    value = rise * (scale * (noise + lean * before) + share * common)
    return value.astype(jnp.float32)


def gaussian(stream_key, shape, deviation, limit, kind=jnp.bfloat16):
    return jnp.clip(deviation * jax.random.normal(stream_key, shape, jnp.float32), -limit, limit).astype(kind)


def setup_inputs(seed: int = 0) -> dict:
    streams_of = jax.random.split(jax.random.key(seed), 3)
    slab = draw_slab(jax.random.fold_in(streams_of[2], 71), 0)
    factor = gaussian(streams_of[1], (D1, RANK), D1 ** -0.5, 0.25, jnp.float32)
    return dict(slab=slab, factor=factor)


def reference(slab, factor):

    def one_comp(block):
        return jnp.einsum('iab,jab->ij', block, block, precision=lax.Precision.HIGHEST)
    grams = lax.map(one_comp, slab)
    gram = jnp.sum(grams, axis=0) / NCOL
    r_factor = jnp.linalg.cholesky(gram).T
    core = jnp.einsum('ir,ciab->crab', factor, slab, precision=lax.Precision.HIGHEST)
    return (r_factor, core)
```

```python
import functools
import jax
import jax.numpy as jnp
from jax import lax
from jax.experimental import pallas as pl
from jax.experimental.pallas import tpu as pltpu
from jax.sharding import PartitionSpec as P

MESH = pl.DeviceIdType.MESH
F32 = jnp.float32
BF16 = jnp.bfloat16


def split(x):
    hi = x.astype(BF16)
    return hi, (x - hi.astype(F32)).astype(BF16)


def nt(a, b):
    return lax.dot_general(a, b, (((1,), (1,)), ((), ())), preferred_element_type=F32)


def nn(a, b):
    return lax.dot_general(a, b, (((1,), (0,)), ((), ())), preferred_element_type=F32)


def exchange_kernel(
    nw, scale, slab, factor, gd, gc, core,
    mine, far, own_h, own_l, far_h, far_l, fac, diag1, diag2, cross,
    half, half_in, dpiece, dpiece_in, quarter, quarter_in, cpiece, cpiece_in,
    core_keep, core_give,
    far_send, far_recv, sib_send, sib_recv, loc_sem,
    half_sems, dw_send, dw_recv, da_send, da_recv, dn_send, dn_recv,
    q_send, q_recv, cw_send, cw_recv, ca_send, ca_recv, cn_send, cn_recv,
    core_sems, keep_sem,
):
    w = lax.axis_index("wide")
    n = lax.axis_index("narrow")
    p, q = n // 2, n % 2
    o, z = 1 - p, 1 - q
    sib = 2 * p + z
    ncomp = slab.shape[0]
    rows = slab.shape[1]

    barrier = pltpu.get_barrier_semaphore()
    for d in range(1, 4):
        pl.semaphore_signal(barrier, inc=1, device_id={"narrow": (n + d) % 4}, device_id_type=MESH)

    @pl.loop(1, nw)
    def _(d):
        pl.semaphore_signal(barrier, inc=1, device_id={"wide": (w + d) % nw}, device_id_type=MESH)

    pl.semaphore_wait(barrier, 3 + nw - 1)

    def remote(src, dst, ssem, rsem, **where):
        return pltpu.make_async_remote_copy(
            src_ref=src, dst_ref=dst, send_sem=ssem, recv_sem=rsem,
            device_id=where, device_id_type=MESH,
        )

    def lane_half(h):
        return pl.ds(pl.multiple_of(h * 128, 128), 128)

    def row_tile(t):
        return pl.ds(pl.multiple_of(t * 8, 8), 8)

    def far_copy(c, m):
        return remote(
            slab.at[c, :, pl.ds(8 * m, 8), lane_half(o)], far.at[q, c],
            far_send.at[c, m], far_recv.at[c, q], narrow=2 * o + m,
        )

    def sib_copy(c, l):
        return remote(
            slab.at[c, :, row_tile(z), pl.ds(128 * l, 128)], mine.at[q, c, l],
            sib_send.at[c, l], sib_recv.at[c, l], narrow=sib,
        )

    def loc_copy(c, l):
        return pltpu.make_async_copy(
            slab.at[c, :, row_tile(q), pl.ds(128 * l, 128)], mine.at[q, c, l], loc_sem.at[c, l]
        )

    for c in range(ncomp):
        far_copy(c, 0).start()
        far_copy(c, 1).start()
        for l in range(2):
            sib_copy(c, l).start()
            loc_copy(c, l).start()

    ft = factor[...].T
    for h in range(2):
        hi, lo = split(ft[:, 256 * h:256 * h + 256])
        fac[h, :64, :] = hi
        fac[h, 64:, :] = lo
    diag1[...] = jnp.zeros_like(diag1)
    diag2[...] = jnp.zeros_like(diag2)
    cross[...] = jnp.zeros_like(cross)

    mine_rows = mine.reshape(2, ncomp, 2, rows * 8, 128)
    far_rows = far.reshape(2, ncomp, rows * 8, 128)

    @pl.loop(0, ncomp)
    def _(c):
        for l in range(2):
            loc_copy(c, l).wait()
            remote(
                mine.at[z, c, l], mine.at[z, c, l], sib_send.at[c, l], sib_recv.at[c, l], narrow=sib
            ).wait_recv()
        for l in range(2):
            for m in range(2):
                for a in range(8):
                    hi, lo = split(mine_rows[m, c, l, pl.ds(a, rows, stride=8), :])
                    own_h[c, l, rows * m:rows * m + rows, 128 * a:128 * a + 128] = hi
                    own_l[c, l, rows * m:rows * m + rows, 128 * a:128 * a + 128] = lo
            diag1[...] += nt(own_h[c, l], own_h[c, l])
            diag2[...] += nt(own_h[c, l], own_l[c, l])

    def scatter_sum(pieces, pieces_in, ssem, rsem):
        def copy(j):
            return remote(pieces.at[j], pieces_in.at[w], ssem.at[j], rsem.at[w], wide=j)

        @pl.loop(1, nw)
        def _(d):
            copy((w + d) % nw).start()

        pieces_in[w] = pieces[w]

        @pl.loop(1, nw)
        def _(d):
            j = (w + d) % nw
            remote(pieces.at[j], pieces_in.at[j], ssem.at[j], rsem.at[j], wide=j).wait_recv()

        @pl.loop(1, nw)
        def _(d):
            copy((w + d) % nw).wait_send()

        total = pieces_in[0]
        for j in range(1, nw):
            total = total + pieces_in[j]
        return total

    def gather_all(full, ssem, rsem):
        def copy(j, slot):
            return remote(full.at[n, slot], full.at[n, slot], ssem.at[j], rsem.at[slot], wide=j)

        @pl.loop(1, nw)
        def _(d):
            copy((w + d) % nw, w).start()

        @pl.loop(1, nw)
        def _(d):
            j = (w + d) % nw
            copy(j, j).wait_recv()

        @pl.loop(1, nw)
        def _(d):
            copy((w + d) % nw, w).wait_send()

    def share_start(full, ssem, rsem):
        for d in range(1, 4):
            k = (n + d) % 4
            remote(full.at[n], full.at[n], ssem.at[k], rsem.at[n], narrow=k).start()

    def share_wait(full, ssem, rsem):
        for d in range(1, 4):
            k = (n + d) % 4
            remote(full.at[k], full.at[k], ssem.at[k], rsem.at[k], narrow=k).wait_recv()
        for d in range(1, 4):
            k = (n + d) % 4
            remote(full.at[n], full.at[n], ssem.at[k], rsem.at[n], narrow=k).wait_send()

    rpp = 128 // nw

    mixed = diag2[...]
    whole = diag1[...] + (mixed + mixed.T)
    half[0] = whole[:128]
    half[1] = whole[128:]
    swap = remote(half.at[z], half_in, half_sems.at[0], half_sems.at[1], narrow=sib)
    swap.start()
    swap.wait()
    part = half[q] + half_in[...]
    for j in range(nw):
        for l in range(2):
            dpiece[j, l] = part[rpp * j:rpp * j + rpp, 128 * l:128 * l + 128]
    gd[n, w] = scatter_sum(dpiece, dpiece_in, dw_send, dw_recv) * scale
    gather_all(gd, da_send, da_recv)
    share_start(gd, dn_send, dn_recv)

    @pl.loop(0, ncomp)
    def _(c):
        for m in range(2):
            remote(
                far.at[m, c], far.at[m, c], far_send.at[c, m], far_recv.at[c, m], narrow=2 * o + m
            ).wait_recv()
        for m in range(2):
            for a in range(8):
                hi, lo = split(far_rows[m, c, pl.ds(a, rows, stride=8), :])
                far_h[rows * m:rows * m + rows, 128 * a:128 * a + 128] = hi
                far_l[rows * m:rows * m + rows, 128 * a:128 * a + 128] = lo
        cross[...] += nt(own_h[c, p], far_h[...]) + (
            nt(own_h[c, p], far_l[...]) + nt(own_l[c, p], far_h[...])
        )
        both = nn(fac[p], own_h[c, p]) + nn(fac[o], far_h[...])
        low = nn(fac[p, :64], own_l[c, p]) + nn(fac[o, :64], far_l[...])
        value = both[:64] + (both[64:] + low)
        keep_rows = core_keep.at[c].reshape(64 * 8, 64)
        give_rows = core_give.at[c].reshape(64 * 8, 64)
        for a in range(8):
            left = value[:, 128 * a:128 * a + 64]
            right = value[:, 128 * a + 64:128 * a + 128]
            keep_rows[pl.ds(a, 64, stride=8), :] = jnp.where(q == 0, left, right)
            give_rows[pl.ds(a, 64, stride=8), :] = jnp.where(q == 0, right, left)

    block = cross[...]
    block = jnp.where(p == 0, block, block.T)
    for k in range(4):
        l, h = k // 2, k % 2
        quarter[k] = block[128 * h:128 * h + 128, 128 * l:128 * l + 128]

    def quarter_copy(k, slot):
        return remote(quarter.at[k], quarter_in.at[slot], q_send.at[k], q_recv.at[slot], narrow=k)

    for d in range(1, 4):
        quarter_copy((n + d) % 4, n).start()
    keep = pltpu.make_async_copy(core_keep, core.at[:, :, row_tile(q), :], keep_sem)
    keep.start()
    give = remote(core_give, core.at[:, :, row_tile(q), :], core_sems.at[0], core_sems.at[1], narrow=sib)
    give.start()
    quarter_in[n] = quarter[n]
    for d in range(1, 4):
        quarter_copy((n + d) % 4, (n + d) % 4).wait_recv()
    for d in range(1, 4):
        quarter_copy((n + d) % 4, n).wait_send()
    part = (quarter_in[0] + quarter_in[1]) + (quarter_in[2] + quarter_in[3])
    for j in range(nw):
        cpiece[j] = part[rpp * j:rpp * j + rpp]
    gc[n, w] = scatter_sum(cpiece, cpiece_in, cw_send, cw_recv) * scale
    gather_all(gc, ca_send, ca_recv)
    share_start(gc, cn_send, cn_recv)
    share_wait(gd, dn_send, dn_recv)
    share_wait(gc, cn_send, cn_recv)

    for c in range(ncomp):
        for m in range(2):
            far_copy(c, m).wait_send()
        for l in range(2):
            sib_copy(c, l).wait_send()
    keep.wait()
    give.wait_send()
    remote(core_give, core.at[:, :, row_tile(z), :], core_sems.at[0], core_sems.at[1], narrow=sib).wait_recv()


def exchange(nw, ncol, slab, factor):
    ncomp, rows, _, _ = slab.shape
    rank = factor.shape[1]
    rpp = 128 // nw
    dma = pltpu.SemaphoreType.DMA
    vmem = pl.BlockSpec(memory_space=pltpu.VMEM)
    anywhere = pl.BlockSpec(memory_space=pl.ANY)
    return pl.pallas_call(
        functools.partial(exchange_kernel, nw, 1.0 / ncol),
        out_shape=(
            jax.ShapeDtypeStruct((4, nw, 2, rpp, 128), F32),
            jax.ShapeDtypeStruct((4, nw, rpp, 128), F32),
            jax.ShapeDtypeStruct((ncomp, rank, 16, 64), F32),
        ),
        in_specs=[anywhere, vmem],
        out_specs=(vmem, vmem, anywhere),
        scratch_shapes=[
            pltpu.VMEM((2, ncomp, 2, rows, 8, 128), F32),
            pltpu.VMEM((2, ncomp, rows, 8, 128), F32),
            pltpu.VMEM((ncomp, 2, 256, 1024), BF16),
            pltpu.VMEM((ncomp, 2, 256, 1024), BF16),
            pltpu.VMEM((256, 1024), BF16),
            pltpu.VMEM((256, 1024), BF16),
            pltpu.VMEM((2, 128, 256), BF16),
            pltpu.VMEM((256, 256), F32),
            pltpu.VMEM((256, 256), F32),
            pltpu.VMEM((256, 256), F32),
            pltpu.VMEM((2, 128, 256), F32),
            pltpu.VMEM((128, 256), F32),
            pltpu.VMEM((nw, 2, rpp, 128), F32),
            pltpu.VMEM((nw, 2, rpp, 128), F32),
            pltpu.VMEM((4, 128, 128), F32),
            pltpu.VMEM((4, 128, 128), F32),
            pltpu.VMEM((nw, rpp, 128), F32),
            pltpu.VMEM((nw, rpp, 128), F32),
            pltpu.VMEM((ncomp, rank, 8, 64), F32),
            pltpu.VMEM((ncomp, rank, 8, 64), F32),
            dma((ncomp, 2)), dma((ncomp, 2)), dma((ncomp, 2)), dma((ncomp, 2)), dma((ncomp, 2)),
            dma((2,)), dma((nw,)), dma((nw,)), dma((nw,)), dma((nw,)), dma((4,)), dma((4,)),
            dma((4,)), dma((4,)), dma((nw,)), dma((nw,)), dma((nw,)), dma((nw,)), dma((4,)), dma((4,)),
            dma((2,)), dma,
        ],
        compiler_params=pltpu.CompilerParams(
            collective_id=0, has_side_effects=True, vmem_limit_bytes=48 * 1024 * 1024
        ),
    )(slab, factor)


def eliminate(work, out, base, lanes0, offset):
    lanes = work.shape[1] // 128
    spot = lax.broadcasted_iota(jnp.int32, (8, 128), 0)

    def spread(x, t):
        return jnp.broadcast_to(x[t:t + 1, :], (8, 128))

    rows = [work[pl.ds(base + 8 * s, 8), :] for s in range(4)]
    tiles = [[r[:, 128 * l:128 * l + 128] for l in range(lanes)] for r in rows]
    for s in range(4):
        tiles[s].append(work[pl.ds(base + 8 * s, 8), pl.ds(lanes0, 128)])
    for s in range(4):
        cols = []
        for u in range(8):
            at = offset + 8 * s + u
            cols.append({
                k: jnp.broadcast_to(tiles[k][lanes][:, at:at + 1], (8, 128)) for k in range(s, 4)
            })
        done = [jnp.zeros((8, 128), F32) for _ in range(lanes)]
        for t in range(8):
            inv = lax.rsqrt(spread(cols[t][s], t))
            line = [spread(x, t) * inv for x in tiles[s]]
            heads = {u: spread(cols[u][s], t) * inv for u in range(t + 1, 8)}
            for l in range(lanes):
                done[l] = jnp.where(spot == t, line[l], done[l])
            for k in range(s, 4):
                m = cols[t][k] * inv
                for u in range(t + 1, 8):
                    cols[u][k] = cols[u][k] - m * heads[u]
                for l in range(lanes + 1):
                    tiles[k][l] = tiles[k][l] - m * line[l]
        for l in range(lanes):
            out[pl.ds(base + 8 * s, 8), 128 * l:128 * l + 128] = done[l]


def tn(a, b):
    return lax.dot_general(
        a, b, (((0,), (0,)), ((), ())), precision=lax.Precision.HIGHEST, preferred_element_type=F32
    )


def factor_kernel(nw, gd, gc, out, work):
    rpp = 128 // nw
    work[...] = jnp.zeros_like(work)
    for k in range(4):
        for j in range(nw):
            for l in range(2):
                lane = 256 * (k // 2) + 128 * l
                work[128 * k + rpp * j:128 * k + rpp * j + rpp, lane:lane + 128] = gd[k, j, l]
            row = 128 * (k % 2) + rpp * j
            lane = 256 + 128 * (k // 2)
            work[row:row + rpp, lane:lane + 128] = gc[k, j]

    @pl.loop(0, 4)
    def _(b):
        top = pl.multiple_of(b * 128, 128)
        for g in range(4):
            base = pl.multiple_of(b * 128 + 32 * g, 32)
            eliminate(work, out, base, top, 32 * g)
            if g < 3:
                line = out[pl.ds(base, 32), :]
                head = out[pl.ds(base, 32), pl.ds(top, 128)]
                work[pl.ds(top, 128), :] -= tn(head, line)

        @pl.loop(b + 1, 4)
        def _(j):
            later = pl.multiple_of(j * 128, 128)
            work[pl.ds(later, 128), :] -= tn(
                out[pl.ds(top, 128), pl.ds(later, 128)], out[pl.ds(top, 128), :]
            )

    row = lax.broadcasted_iota(jnp.int32, (512, 512), 0)
    col = lax.broadcasted_iota(jnp.int32, (512, 512), 1)
    out[...] = jnp.where(col >= row, out[...], 0.0)


def upper_factor(nw, gd, gc):
    vmem = pl.BlockSpec(memory_space=pltpu.VMEM)
    return pl.pallas_call(
        functools.partial(factor_kernel, nw),
        out_shape=jax.ShapeDtypeStruct((512, 512), F32),
        in_specs=[vmem, vmem],
        out_specs=vmem,
        scratch_shapes=[pltpu.VMEM((512, 512), F32)],
        compiler_params=pltpu.CompilerParams(vmem_limit_bytes=32 * 1024 * 1024),
    )(gd, gc)


def on_device(nw, slab, factor):
    ncol = slab.shape[0] * slab.shape[2] * nw * slab.shape[3]
    gd, gc, core = exchange(nw, ncol, slab, factor)
    return upper_factor(nw, gd, gc), core


def solution(mesh):
    return jax.shard_map(
        functools.partial(on_device, mesh.shape["wide"]),
        mesh=mesh,
        in_specs=(P(None, "narrow", "wide", None), P()),
        out_specs=(P(), P(None, None, "wide", "narrow")),
        check_vma=False,
    )
```

```python
import functools
import jax
import jax.numpy as jnp
from jax import lax
from jax.experimental import pallas as pl
from jax.experimental.pallas import tpu as pltpu
from jax.sharding import PartitionSpec as P

MESH = pl.DeviceIdType.MESH
F32 = jnp.float32
BF16 = jnp.bfloat16


def split(x):
    hi = x.astype(BF16)
    return hi, (x - hi.astype(F32)).astype(BF16)


def nt(a, b):
    return lax.dot_general(a, b, (((1,), (1,)), ((), ())), preferred_element_type=F32)


def nn(a, b):
    return lax.dot_general(a, b, (((1,), (0,)), ((), ())), preferred_element_type=F32)


def exchange_kernel(
    nw, scale, slab, ft, gd, gc, lead, core,
    mine, far, own_h, own_l, far_h, far_l, fac, diag1, diag2, cross,
    half, half_in, dpiece, dpiece_in, quarter, quarter_in, cpiece, cpiece_in,
    core_keep, core_give, work,
    far_send, far_recv, sib_send, sib_recv, loc_sem,
    half_sems, dw_send, dw_recv, da_send, da_recv, dn_send, dn_recv,
    q_send, q_recv, cw_send, cw_recv, ca_send, ca_recv, cn_send, cn_recv,
    core_sems, keep_sem,
):
    w = lax.axis_index("wide")
    n = lax.axis_index("narrow")
    p, q = n // 2, n % 2
    o, z = 1 - p, 1 - q
    sib = 2 * p + z
    ncomp = slab.shape[0]
    rows = slab.shape[1]

    barrier = pltpu.get_barrier_semaphore()
    for d in range(1, 4):
        pl.semaphore_signal(barrier, inc=1, device_id={"narrow": (n + d) % 4}, device_id_type=MESH)

    @pl.loop(1, nw)
    def _(d):
        pl.semaphore_signal(barrier, inc=1, device_id={"wide": (w + d) % nw}, device_id_type=MESH)

    pl.semaphore_wait(barrier, 3 + nw - 1)

    def remote(src, dst, ssem, rsem, **where):
        return pltpu.make_async_remote_copy(
            src_ref=src, dst_ref=dst, send_sem=ssem, recv_sem=rsem,
            device_id=where, device_id_type=MESH,
        )

    def lane_half(h):
        return pl.ds(pl.multiple_of(h * 128, 128), 128)

    def row_tile(t):
        return pl.ds(pl.multiple_of(t * 8, 8), 8)

    def far_copy(c, m):
        return remote(
            slab.at[c, :, pl.ds(8 * m, 8), lane_half(o)], far.at[q, c],
            far_send.at[c, m], far_recv.at[c, q], narrow=2 * o + m,
        )

    def sib_copy(c, l):
        return remote(
            slab.at[c, :, row_tile(z), pl.ds(128 * l, 128)], mine.at[q, c, l],
            sib_send.at[c, l], sib_recv.at[c, l], narrow=sib,
        )

    def loc_copy(c, l):
        return pltpu.make_async_copy(
            slab.at[c, :, row_tile(q), pl.ds(128 * l, 128)], mine.at[q, c, l], loc_sem.at[c, l]
        )

    last = ncomp - 1
    for c in range(ncomp):
        if c < last:
            far_copy(c, 0).start()
            far_copy(c, 1).start()
        for l in range(2):
            sib_copy(c, l).start()
            loc_copy(c, l).start()

    for h in range(2):
        hi, lo = split(ft[:, 256 * h:256 * h + 256])
        fac[h, :64, :] = hi
        fac[h, 64:, :] = lo
    diag1[...] = jnp.zeros_like(diag1)
    diag2[...] = jnp.zeros_like(diag2)
    cross[...] = jnp.zeros_like(cross)

    mine_rows = mine.reshape(2, ncomp, 2, rows * 8, 128)
    far_rows = far.reshape(2, ncomp, rows * 8, 128)

    @pl.loop(0, ncomp)
    def _(c):
        for l in range(2):
            loc_copy(c, l).wait()
            remote(
                mine.at[z, c, l], mine.at[z, c, l], sib_send.at[c, l], sib_recv.at[c, l], narrow=sib
            ).wait_recv()
        for l in range(2):
            for m in range(2):
                for a in range(8):
                    hi, lo = split(mine_rows[m, c, l, pl.ds(a, rows, stride=8), :])
                    own_h[c, l, rows * m:rows * m + rows, 128 * a:128 * a + 128] = hi
                    own_l[c, l, rows * m:rows * m + rows, 128 * a:128 * a + 128] = lo
            diag1[...] += nt(own_h[c, l], own_h[c, l])
            diag2[...] += nt(own_h[c, l], own_l[c, l])

    def scatter_sum(pieces, pieces_in, ssem, rsem):
        def copy(j):
            return remote(pieces.at[j], pieces_in.at[w], ssem.at[j], rsem.at[w], wide=j)

        @pl.loop(1, nw)
        def _(d):
            copy((w + d) % nw).start()

        pieces_in[w] = pieces[w]

        @pl.loop(1, nw)
        def _(d):
            j = (w + d) % nw
            remote(pieces.at[j], pieces_in.at[j], ssem.at[j], rsem.at[j], wide=j).wait_recv()

        @pl.loop(1, nw)
        def _(d):
            copy((w + d) % nw).wait_send()

        total = pieces_in[0]
        for j in range(1, nw):
            total = total + pieces_in[j]
        return total

    def gather_all(full, ssem, rsem):
        def copy(j, slot):
            return remote(full.at[n, slot], full.at[n, slot], ssem.at[j], rsem.at[slot], wide=j)

        @pl.loop(1, nw)
        def _(d):
            copy((w + d) % nw, w).start()

        @pl.loop(1, nw)
        def _(d):
            j = (w + d) % nw
            copy(j, j).wait_recv()

        @pl.loop(1, nw)
        def _(d):
            copy((w + d) % nw, w).wait_send()

    def share_copy(full, ssem, rsem, i, slot, k):
        return remote(full.at[slot], full.at[slot], ssem.at[i], rsem.at[slot], narrow=k)

    rpp = 128 // nw

    mixed = diag2[...]
    whole = diag1[...] + (mixed + mixed.T)
    half[0] = whole[:128]
    half[1] = whole[128:]
    swap = remote(half.at[z], half_in, half_sems.at[0], half_sems.at[1], narrow=sib)
    swap.start()
    swap.wait()
    part = half[q] + half_in[...]
    for j in range(nw):
        for l in range(2):
            dpiece[j, l] = part[rpp * j:rpp * j + rpp, 128 * l:128 * l + 128]
    gd[n, w] = scatter_sum(dpiece, dpiece_in, dw_send, dw_recv) * scale
    gather_all(gd, da_send, da_recv)
    far_same = 2 * o + q
    far_cross = 2 * o + z
    share_copy(gd, dn_send, dn_recv, 0, n, sib).start()
    share_copy(gd, dn_send, dn_recv, 1, n, far_same).start()
    far_copy(last, 0).start()
    far_copy(last, 1).start()

    def add_cross(c):
        for m in range(2):
            remote(
                far.at[m, c], far.at[m, c], far_send.at[c, m], far_recv.at[c, m], narrow=2 * o + m
            ).wait_recv()
        for m in range(2):
            for a in range(8):
                hi, lo = split(far_rows[m, c, pl.ds(a, rows, stride=8), :])
                far_h[rows * m:rows * m + rows, 128 * a:128 * a + 128] = hi
                far_l[rows * m:rows * m + rows, 128 * a:128 * a + 128] = lo
        cross[...] += nt(own_h[c, p], far_h[...]) + (
            nt(own_h[c, p], far_l[...]) + nt(own_l[c, p], far_h[...])
        )

    def make_core(c):
        both = nn(fac[p], own_h[c, p]) + nn(fac[o], far_h[...])
        low = nn(fac[p, :64], own_l[c, p]) + nn(fac[o, :64], far_l[...])
        value = both[:64] + (both[64:] + low)
        keep_rows = core_keep.at[c].reshape(64 * 8, 64)
        give_rows = core_give.at[c].reshape(64 * 8, 64)
        for a in range(8):
            left = value[:, 128 * a:128 * a + 64]
            right = value[:, 128 * a + 64:128 * a + 128]
            keep_rows[pl.ds(a, 64, stride=8), :] = jnp.where(q == 0, left, right)
            give_rows[pl.ds(a, 64, stride=8), :] = jnp.where(q == 0, right, left)

    early = ncomp // 2

    @pl.loop(0, early)
    def _(c):
        add_cross(c)
        make_core(c)

    share_copy(gd, dn_send, dn_recv, 0, sib, sib).wait_recv()
    share_copy(gd, dn_send, dn_recv, 1, far_same, far_same).wait_recv()
    share_copy(gd, dn_send, dn_recv, 2, far_same, sib).start()
    share_copy(gd, dn_send, dn_recv, 2, far_cross, sib).wait_recv()

    for k in range(2):
        for j in range(nw):
            for l in range(2):
                work[128 * k + rpp * j:128 * k + rpp * j + rpp, 128 * l:128 * l + 128] = gd[k, j, l]
    row = lax.broadcasted_iota(jnp.int32, (256, 256), 0)
    col = lax.broadcasted_iota(jnp.int32, (256, 256), 1)
    work[:, 256:] = (row == col).astype(F32)

    @pl.loop(0, 2)
    def _(b):
        top = pl.multiple_of(b * 128, 128)
        for g in range(4):
            base = pl.multiple_of(b * 128 + 32 * g, 32)
            eliminate(work, lead, base, top, 32 * g)
            if g < 3:
                work[pl.ds(top, 128), :] -= tn(
                    lead[pl.ds(base, 32), pl.ds(top, 128)], lead[pl.ds(base, 32), :]
                )

        @pl.when(b == 0)
        def _():
            work[128:, :] -= tn(lead[:128, 128:256], lead[:128, :])

    @pl.loop(early, last)
    def _(c):
        add_cross(c)
        make_core(c)

    add_cross(last)
    block = cross[...]
    block = jnp.where(p == 0, block, block.T)
    for k in range(4):
        l, h = k // 2, k % 2
        quarter[k] = block[128 * h:128 * h + 128, 128 * l:128 * l + 128]

    def quarter_copy(k, slot):
        return remote(quarter.at[k], quarter_in.at[slot], q_send.at[k], q_recv.at[slot], narrow=k)

    for d in range(1, 4):
        quarter_copy((n + d) % 4, n).start()
    make_core(last)
    keep = pltpu.make_async_copy(core_keep, core.at[:, :, row_tile(q), :], keep_sem)
    keep.start()
    give = remote(core_give, core.at[:, :, row_tile(q), :], core_sems.at[0], core_sems.at[1], narrow=sib)
    give.start()
    quarter_in[n] = quarter[n]
    for d in range(1, 4):
        quarter_copy((n + d) % 4, (n + d) % 4).wait_recv()
    for d in range(1, 4):
        quarter_copy((n + d) % 4, n).wait_send()
    part = (quarter_in[0] + quarter_in[1]) + (quarter_in[2] + quarter_in[3])
    for j in range(nw):
        cpiece[j] = part[rpp * j:rpp * j + rpp]
    gc[n, w] = scatter_sum(cpiece, cpiece_in, cw_send, cw_recv) * scale
    gather_all(gc, ca_send, ca_recv)
    for d in range(1, 4):
        k = (n + d) % 4
        share_copy(gc, cn_send, cn_recv, d, n, k).start()
    for d in range(1, 4):
        k = (n + d) % 4
        share_copy(gc, cn_send, cn_recv, d, k, k).wait_recv()
    for d in range(1, 4):
        share_copy(gc, cn_send, cn_recv, d, n, (n + d) % 4).wait_send()
    share_copy(gd, dn_send, dn_recv, 0, n, sib).wait_send()
    share_copy(gd, dn_send, dn_recv, 1, n, far_same).wait_send()
    share_copy(gd, dn_send, dn_recv, 2, far_same, sib).wait_send()

    for c in range(ncomp):
        for m in range(2):
            far_copy(c, m).wait_send()
        for l in range(2):
            sib_copy(c, l).wait_send()
    keep.wait()
    give.wait_send()
    remote(core_give, core.at[:, :, row_tile(z), :], core_sems.at[0], core_sems.at[1], narrow=sib).wait_recv()


def exchange(nw, ncol, slab, ft):
    ncomp, rows, _, _ = slab.shape
    rank = ft.shape[0]
    rpp = 128 // nw
    dma = pltpu.SemaphoreType.DMA
    vmem = pl.BlockSpec(memory_space=pltpu.VMEM)
    anywhere = pl.BlockSpec(memory_space=pl.ANY)
    return pl.pallas_call(
        functools.partial(exchange_kernel, nw, 1.0 / ncol),
        out_shape=(
            jax.ShapeDtypeStruct((4, nw, 2, rpp, 128), F32),
            jax.ShapeDtypeStruct((4, nw, rpp, 128), F32),
            jax.ShapeDtypeStruct((256, 512), F32),
            jax.ShapeDtypeStruct((ncomp, rank, 16, 64), F32),
        ),
        in_specs=[anywhere, vmem],
        out_specs=(vmem, vmem, vmem, anywhere),
        scratch_shapes=[
            pltpu.VMEM((2, ncomp, 2, rows, 8, 128), F32),
            pltpu.VMEM((2, ncomp, rows, 8, 128), F32),
            pltpu.VMEM((ncomp, 2, 256, 1024), BF16),
            pltpu.VMEM((ncomp, 2, 256, 1024), BF16),
            pltpu.VMEM((256, 1024), BF16),
            pltpu.VMEM((256, 1024), BF16),
            pltpu.VMEM((2, 128, 256), BF16),
            pltpu.VMEM((256, 256), F32),
            pltpu.VMEM((256, 256), F32),
            pltpu.VMEM((256, 256), F32),
            pltpu.VMEM((2, 128, 256), F32),
            pltpu.VMEM((128, 256), F32),
            pltpu.VMEM((nw, 2, rpp, 128), F32),
            pltpu.VMEM((nw, 2, rpp, 128), F32),
            pltpu.VMEM((4, 128, 128), F32),
            pltpu.VMEM((4, 128, 128), F32),
            pltpu.VMEM((nw, rpp, 128), F32),
            pltpu.VMEM((nw, rpp, 128), F32),
            pltpu.VMEM((ncomp, rank, 8, 64), F32),
            pltpu.VMEM((ncomp, rank, 8, 64), F32),
            pltpu.VMEM((256, 512), F32),
            dma((ncomp, 2)), dma((ncomp, 2)), dma((ncomp, 2)), dma((ncomp, 2)), dma((ncomp, 2)),
            dma((2,)), dma((nw,)), dma((nw,)), dma((nw,)), dma((nw,)), dma((4,)), dma((4,)),
            dma((4,)), dma((4,)), dma((nw,)), dma((nw,)), dma((nw,)), dma((nw,)), dma((4,)), dma((4,)),
            dma((2,)), dma,
        ],
        compiler_params=pltpu.CompilerParams(
            collective_id=0, has_side_effects=True, vmem_limit_bytes=48 * 1024 * 1024
        ),
    )(slab, ft)


def eliminate(work, out, base, lanes0, offset):
    lanes = work.shape[1] // 128
    spot = lax.broadcasted_iota(jnp.int32, (8, 128), 0)

    def spread(x, t):
        return jnp.broadcast_to(x[t:t + 1, :], (8, 128))

    rows = [work[pl.ds(base + 8 * s, 8), :] for s in range(4)]
    tiles = [[r[:, 128 * l:128 * l + 128] for l in range(lanes)] for r in rows]
    for s in range(4):
        tiles[s].append(work[pl.ds(base + 8 * s, 8), pl.ds(lanes0, 128)])
    for s in range(4):
        cols = []
        for u in range(8):
            at = offset + 8 * s + u
            cols.append({
                k: jnp.broadcast_to(tiles[k][lanes][:, at:at + 1], (8, 128)) for k in range(s, 4)
            })
        done = [jnp.zeros((8, 128), F32) for _ in range(lanes)]
        for t in range(8):
            inv = lax.rsqrt(spread(cols[t][s], t))
            line = [spread(x, t) * inv for x in tiles[s]]
            heads = {u: spread(cols[u][s], t) * inv for u in range(t + 1, 8)}
            for l in range(lanes):
                done[l] = jnp.where(spot == t, line[l], done[l])
            for k in range(s, 4):
                m = cols[t][k] * inv
                for u in range(t + 1, 8):
                    cols[u][k] = cols[u][k] - m * heads[u]
                for l in range(lanes + 1):
                    tiles[k][l] = tiles[k][l] - m * line[l]
        for l in range(lanes):
            out[pl.ds(base + 8 * s, 8), 128 * l:128 * l + 128] = done[l]


def tn(a, b):
    return lax.dot_general(
        a, b, (((0,), (0,)), ((), ())), precision=lax.Precision.HIGHEST, preferred_element_type=F32
    )


def finish_kernel(nw, gd, gc, lead, core_in, out, core_out, g01, work, tail, sem):
    move = pltpu.make_async_copy(core_in, core_out, sem)
    move.start()
    rpp = 128 // nw
    for k in range(4):
        for j in range(nw):
            row = 128 * (k % 2) + rpp * j
            lane = 128 * (k // 2)
            g01[row:row + rpp, lane:lane + 128] = gc[k, j]
            if k >= 2:
                for l in range(2):
                    work[row:row + rpp, 128 * l:128 * l + 128] = gd[k, j, l]
    row = lax.broadcasted_iota(jnp.int32, (256, 256), 0)
    col = lax.broadcasted_iota(jnp.int32, (256, 256), 1)
    upper = col >= row
    out[:256, :256] = jnp.where(upper, lead[:, :256], 0.0)
    out[256:, :256] = jnp.zeros((256, 256), F32)
    side = lax.dot_general(
        lead[:, 256:], g01[...], (((1,), (0,)), ((), ())),
        precision=lax.Precision.HIGHEST, preferred_element_type=F32,
    )
    out[:256, 256:] = side
    work[...] -= tn(side, side)
    for b in range(2):
        top = 128 * b
        for g in range(4):
            base = top + 32 * g
            eliminate(work, tail, base, top, 32 * g)
            if g < 3:
                work[base + 32:top + 128, top:] -= tn(
                    tail[base:base + 32, base + 32:top + 128], tail[base:base + 32, top:]
                )
        if b == 0:
            work[128:, 128:] -= tn(tail[:128, 128:], tail[:128, 128:])
    out[256:, 256:] = jnp.where(upper, tail[...], 0.0)
    move.wait()


def finish(nw, gd, gc, lead, core):
    vmem = pl.BlockSpec(memory_space=pltpu.VMEM)
    anywhere = pl.BlockSpec(memory_space=pl.ANY)
    return pl.pallas_call(
        functools.partial(finish_kernel, nw),
        out_shape=(
            jax.ShapeDtypeStruct((512, 512), F32),
            jax.ShapeDtypeStruct(core.shape, F32),
        ),
        in_specs=[vmem, vmem, vmem, anywhere],
        out_specs=(vmem, anywhere),
        scratch_shapes=[
            pltpu.VMEM((256, 256), F32),
            pltpu.VMEM((256, 256), F32),
            pltpu.VMEM((256, 256), F32),
            pltpu.SemaphoreType.DMA,
        ],
        compiler_params=pltpu.CompilerParams(vmem_limit_bytes=32 * 1024 * 1024),
    )(gd, gc, lead, core)


def on_device(nw, slab, factor):
    ncol = slab.shape[0] * slab.shape[2] * nw * slab.shape[3]
    return finish(nw, *exchange(nw, ncol, slab, factor.T))


def solution(mesh):
    return jax.shard_map(
        functools.partial(on_device, mesh.shape["wide"]),
        mesh=mesh,
        in_specs=(P(None, "narrow", "wide", None), P()),
        out_specs=(P(), P(None, None, "wide", "narrow")),
        check_vma=False,
    )
```

```python
import functools
import jax
import jax.numpy as jnp
from jax import lax
from jax.experimental import pallas as pl
from jax.experimental.pallas import tpu as pltpu
from jax.sharding import PartitionSpec as P

MESH = pl.DeviceIdType.MESH
F32 = jnp.float32
BF16 = jnp.bfloat16


def split(x):
    hi = x.astype(BF16)
    return hi, (x - hi.astype(F32)).astype(BF16)


def nt(a, b):
    return lax.dot_general(a, b, (((1,), (1,)), ((), ())), preferred_element_type=F32)


def nn(a, b):
    return lax.dot_general(a, b, (((1,), (0,)), ((), ())), preferred_element_type=F32)


def exchange_kernel(
    nw, scale, slab, ft, gd, gc, lead, core,
    mine, far, own_h, own_l, far_h, far_l, fac, diag1, diag2, cross,
    half, half_in, dpiece, dpiece_in, quarter, quarter_in, cpiece, cpiece_in,
    core_keep, core_give, work,
    far_send, far_recv, sib_send, sib_recv, loc_sem,
    half_sems, dw_send, dw_recv, da_send, da_recv, dn_send, dn_recv,
    q_send, q_recv, cw_send, cw_recv, ca_send, ca_recv, cn_send, cn_recv,
    core_sems, keep_sem,
):
    w = lax.axis_index("wide")
    n = lax.axis_index("narrow")
    p, q = n // 2, n % 2
    o, z = 1 - p, 1 - q
    sib = 2 * p + z
    ncomp = slab.shape[0]
    rows = slab.shape[1]

    barrier = pltpu.get_barrier_semaphore()
    for d in range(1, 4):
        pl.semaphore_signal(barrier, inc=1, device_id={"narrow": (n + d) % 4}, device_id_type=MESH)

    @pl.loop(1, nw)
    def _(d):
        pl.semaphore_signal(barrier, inc=1, device_id={"wide": (w + d) % nw}, device_id_type=MESH)

    pl.semaphore_wait(barrier, 3 + nw - 1)

    def remote(src, dst, ssem, rsem, **where):
        return pltpu.make_async_remote_copy(
            src_ref=src, dst_ref=dst, send_sem=ssem, recv_sem=rsem,
            device_id=where, device_id_type=MESH,
        )

    def lane_half(h):
        return pl.ds(pl.multiple_of(h * 128, 128), 128)

    def row_tile(t):
        return pl.ds(pl.multiple_of(t * 8, 8), 8)

    def far_copy(c, m):
        return remote(
            slab.at[c, :, pl.ds(8 * m, 8), lane_half(o)], far.at[q, c],
            far_send.at[c, m], far_recv.at[c, q], narrow=2 * o + m,
        )

    def sib_copy(c, l):
        return remote(
            slab.at[c, :, row_tile(z), pl.ds(128 * l, 128)], mine.at[q, c, l],
            sib_send.at[c, l], sib_recv.at[c, l], narrow=sib,
        )

    def loc_copy(c, l):
        return pltpu.make_async_copy(
            slab.at[c, :, row_tile(q), pl.ds(128 * l, 128)], mine.at[q, c, l], loc_sem.at[c, l]
        )

    last = ncomp - 1
    early = ncomp // 2

    def far_start(first, stop):
        for c in range(first, stop):
            far_copy(c, 0).start()
            far_copy(c, 1).start()

    far_start(0, 1)
    for c in range(ncomp):
        for l in range(2):
            sib_copy(c, l).start()
            loc_copy(c, l).start()
    far_start(1, early)

    for h in range(2):
        hi, lo = split(ft[:, 256 * h:256 * h + 256])
        fac[h, :64, :] = hi
        fac[h, 64:, :] = lo
    diag1[...] = jnp.zeros_like(diag1)
    diag2[...] = jnp.zeros_like(diag2)
    cross[...] = jnp.zeros_like(cross)

    mine_rows = mine.reshape(2, ncomp, 2, rows * 8, 128)
    far_rows = far.reshape(2, ncomp, rows * 8, 128)

    @pl.loop(0, ncomp)
    def _(c):
        for l in range(2):
            loc_copy(c, l).wait()
            remote(
                mine.at[z, c, l], mine.at[z, c, l], sib_send.at[c, l], sib_recv.at[c, l], narrow=sib
            ).wait_recv()
        for l in range(2):
            for m in range(2):
                for a in range(8):
                    hi, lo = split(mine_rows[m, c, l, pl.ds(a, rows, stride=8), :])
                    own_h[c, l, rows * m:rows * m + rows, 128 * a:128 * a + 128] = hi
                    own_l[c, l, rows * m:rows * m + rows, 128 * a:128 * a + 128] = lo
            diag1[...] += nt(own_h[c, l], own_h[c, l])
            diag2[...] += nt(own_h[c, l], own_l[c, l])

    def scatter_sum(pieces, pieces_in, ssem, rsem):
        def copy(j):
            return remote(pieces.at[j], pieces_in.at[w], ssem.at[j], rsem.at[w], wide=j)

        @pl.loop(1, nw)
        def _(d):
            copy((w + d) % nw).start()

        pieces_in[w] = pieces[w]

        @pl.loop(1, nw)
        def _(d):
            j = (w + d) % nw
            remote(pieces.at[j], pieces_in.at[j], ssem.at[j], rsem.at[j], wide=j).wait_recv()

        @pl.loop(1, nw)
        def _(d):
            copy((w + d) % nw).wait_send()

        total = pieces_in[0]
        for j in range(1, nw):
            total = total + pieces_in[j]
        return total

    def gather_all(full, ssem, rsem):
        def copy(j, slot):
            return remote(full.at[n, slot], full.at[n, slot], ssem.at[j], rsem.at[slot], wide=j)

        @pl.loop(1, nw)
        def _(d):
            copy((w + d) % nw, w).start()

        @pl.loop(1, nw)
        def _(d):
            j = (w + d) % nw
            copy(j, j).wait_recv()

        @pl.loop(1, nw)
        def _(d):
            copy((w + d) % nw, w).wait_send()

    def share_copy(i, slot, k, then):
        def part(l):
            block = gd.at[slot, :, l]
            return remote(block, block, dn_send.at[i, l], dn_recv.at[slot, l], narrow=k)

        then(part(1))

        @pl.when(slot % 2 == 0)
        def _():
            then(part(0))

    def start(copy):
        copy.start()

    def arrived(copy):
        copy.wait_recv()

    def sent(copy):
        copy.wait_send()

    def cross_share(i, slot, k):
        return remote(gc.at[slot], gc.at[slot], cn_send.at[i], cn_recv.at[slot], narrow=k)

    rpp = 128 // nw

    mixed = diag2[...]
    whole = diag1[...] + (mixed + mixed.T)
    half[0] = whole[:128]
    half[1] = whole[128:]
    swap = remote(half.at[z], half_in, half_sems.at[0], half_sems.at[1], narrow=sib)
    swap.start()
    swap.wait()
    part = half[q] + half_in[...]
    for j in range(nw):
        for l in range(2):
            dpiece[j, l] = part[rpp * j:rpp * j + rpp, 128 * l:128 * l + 128]
    gd[n, w] = scatter_sum(dpiece, dpiece_in, dw_send, dw_recv) * scale
    gather_all(gd, da_send, da_recv)
    far_same = 2 * o + q
    far_cross = 2 * o + z
    share_copy(1, n, far_same, start)
    share_copy(0, n, sib, start)
    far_start(early, ncomp)

    def add_cross(c):
        for m in range(2):
            remote(
                far.at[m, c], far.at[m, c], far_send.at[c, m], far_recv.at[c, m], narrow=2 * o + m
            ).wait_recv()
            here = slice(rows * m, rows * m + rows)
            for a in range(8):
                hi, lo = split(far_rows[m, c, pl.ds(a, rows, stride=8), :])
                far_h[here, 128 * a:128 * a + 128] = hi
                far_l[here, 128 * a:128 * a + 128] = lo
            cross[:, here] += nt(own_h[c, p], far_h[here, :]) + (
                nt(own_h[c, p], far_l[here, :]) + nt(own_l[c, p], far_h[here, :])
            )

    def make_core(c):
        both = nn(fac[p], own_h[c, p]) + nn(fac[o], far_h[...])
        low = nn(fac[p, :64], own_l[c, p]) + nn(fac[o, :64], far_l[...])
        value = both[:64] + (both[64:] + low)
        keep_rows = core_keep.at[c].reshape(64 * 8, 64)
        give_rows = core_give.at[c].reshape(64 * 8, 64)
        for a in range(8):
            left = value[:, 128 * a:128 * a + 64]
            right = value[:, 128 * a + 64:128 * a + 128]
            keep_rows[pl.ds(a, 64, stride=8), :] = jnp.where(q == 0, left, right)
            give_rows[pl.ds(a, 64, stride=8), :] = jnp.where(q == 0, right, left)

    @pl.loop(0, early)
    def _(c):
        add_cross(c)
        make_core(c)

    share_copy(0, sib, sib, arrived)
    share_copy(1, far_same, far_same, arrived)
    share_copy(2, far_same, sib, start)
    share_copy(2, far_cross, sib, arrived)

    for k in range(2):
        for j in range(nw):
            for l in range(k, 2):
                work[128 * k + rpp * j:128 * k + rpp * j + rpp, 128 * l:128 * l + 128] = gd[k, j, l]
    work[128:, :128] = jnp.zeros((128, 128), F32)
    row = lax.broadcasted_iota(jnp.int32, (256, 256), 0)
    col = lax.broadcasted_iota(jnp.int32, (256, 256), 1)
    work[:, 256:] = (row == col).astype(F32)

    @pl.loop(0, 2)
    def _(b):
        top = pl.multiple_of(b * 128, 128)
        for g in range(4):
            base = pl.multiple_of(b * 128 + 32 * g, 32)
            eliminate(work, lead, base, top, 32 * g)
            if g < 3:
                work[pl.ds(top, 128), :] -= tn(
                    lead[pl.ds(base, 32), pl.ds(top, 128)], lead[pl.ds(base, 32), :]
                )

        @pl.when(b == 0)
        def _():
            work[128:, :] -= tn(lead[:128, 128:256], lead[:128, :])

    @pl.loop(early, last)
    def _(c):
        add_cross(c)
        make_core(c)

    add_cross(last)
    block = cross[...]
    block = jnp.where(p == 0, block, block.T)
    for k in range(4):
        l, h = k // 2, k % 2
        quarter[k] = block[128 * h:128 * h + 128, 128 * l:128 * l + 128]

    def quarter_copy(k, slot):
        return remote(quarter.at[k], quarter_in.at[slot], q_send.at[k], q_recv.at[slot], narrow=k)

    for d in range(1, 4):
        quarter_copy((n + d) % 4, n).start()
    make_core(last)
    keep = pltpu.make_async_copy(core_keep, core.at[:, :, row_tile(q), :], keep_sem)
    keep.start()
    give = remote(core_give, core.at[:, :, row_tile(q), :], core_sems.at[0], core_sems.at[1], narrow=sib)
    give.start()
    quarter_in[n] = quarter[n]
    for d in range(1, 4):
        quarter_copy((n + d) % 4, (n + d) % 4).wait_recv()
    for d in range(1, 4):
        quarter_copy((n + d) % 4, n).wait_send()
    part = (quarter_in[0] + quarter_in[1]) + (quarter_in[2] + quarter_in[3])
    for j in range(nw):
        cpiece[j] = part[rpp * j:rpp * j + rpp]
    gc[n, w] = scatter_sum(cpiece, cpiece_in, cw_send, cw_recv) * scale
    gather_all(gc, ca_send, ca_recv)
    for d in range(1, 4):
        k = (n + d) % 4
        cross_share(d, n, k).start()
    for d in range(1, 4):
        k = (n + d) % 4
        cross_share(d, k, k).wait_recv()
    for d in range(1, 4):
        cross_share(d, n, (n + d) % 4).wait_send()
    share_copy(0, n, sib, sent)
    share_copy(1, n, far_same, sent)
    share_copy(2, far_same, sib, sent)

    for c in range(ncomp):
        for m in range(2):
            far_copy(c, m).wait_send()
        for l in range(2):
            sib_copy(c, l).wait_send()
    keep.wait()
    give.wait_send()
    remote(core_give, core.at[:, :, row_tile(z), :], core_sems.at[0], core_sems.at[1], narrow=sib).wait_recv()


def exchange(nw, ncol, slab, ft):
    ncomp, rows, _, _ = slab.shape
    rank = ft.shape[0]
    rpp = 128 // nw
    dma = pltpu.SemaphoreType.DMA
    vmem = pl.BlockSpec(memory_space=pltpu.VMEM)
    anywhere = pl.BlockSpec(memory_space=pl.ANY)
    return pl.pallas_call(
        functools.partial(exchange_kernel, nw, 1.0 / ncol),
        out_shape=(
            jax.ShapeDtypeStruct((4, nw, 2, rpp, 128), F32),
            jax.ShapeDtypeStruct((4, nw, rpp, 128), F32),
            jax.ShapeDtypeStruct((256, 512), F32),
            jax.ShapeDtypeStruct((ncomp, rank, 16, 64), F32),
        ),
        in_specs=[anywhere, vmem],
        out_specs=(vmem, vmem, vmem, anywhere),
        scratch_shapes=[
            pltpu.VMEM((2, ncomp, 2, rows, 8, 128), F32),
            pltpu.VMEM((2, ncomp, rows, 8, 128), F32),
            pltpu.VMEM((ncomp, 2, 256, 1024), BF16),
            pltpu.VMEM((ncomp, 2, 256, 1024), BF16),
            pltpu.VMEM((256, 1024), BF16),
            pltpu.VMEM((256, 1024), BF16),
            pltpu.VMEM((2, 128, 256), BF16),
            pltpu.VMEM((256, 256), F32),
            pltpu.VMEM((256, 256), F32),
            pltpu.VMEM((256, 256), F32),
            pltpu.VMEM((2, 128, 256), F32),
            pltpu.VMEM((128, 256), F32),
            pltpu.VMEM((nw, 2, rpp, 128), F32),
            pltpu.VMEM((nw, 2, rpp, 128), F32),
            pltpu.VMEM((4, 128, 128), F32),
            pltpu.VMEM((4, 128, 128), F32),
            pltpu.VMEM((nw, rpp, 128), F32),
            pltpu.VMEM((nw, rpp, 128), F32),
            pltpu.VMEM((ncomp, rank, 8, 64), F32),
            pltpu.VMEM((ncomp, rank, 8, 64), F32),
            pltpu.VMEM((256, 512), F32),
            dma((ncomp, 2)), dma((ncomp, 2)), dma((ncomp, 2)), dma((ncomp, 2)), dma((ncomp, 2)),
            dma((2,)), dma((nw,)), dma((nw,)), dma((nw,)), dma((nw,)), dma((3, 2)), dma((4, 2)),
            dma((4,)), dma((4,)), dma((nw,)), dma((nw,)), dma((nw,)), dma((nw,)), dma((4,)), dma((4,)),
            dma((2,)), dma,
        ],
        compiler_params=pltpu.CompilerParams(
            collective_id=0, has_side_effects=True, vmem_limit_bytes=48 * 1024 * 1024
        ),
    )(slab, ft)


def eliminate(work, out, base, lanes0, offset):
    lanes = work.shape[1] // 128
    spot = lax.broadcasted_iota(jnp.int32, (8, 128), 0)

    def spread(x, t):
        return jnp.broadcast_to(x[t:t + 1, :], (8, 128))

    rows = [work[pl.ds(base + 8 * s, 8), :] for s in range(4)]
    tiles = [[r[:, 128 * l:128 * l + 128] for l in range(lanes)] for r in rows]
    for s in range(4):
        tiles[s].append(work[pl.ds(base + 8 * s, 8), pl.ds(lanes0, 128)])
    for s in range(4):
        def column(u, k):
            at = offset + 8 * s + u
            return jnp.broadcast_to(tiles[k][lanes][:, at:at + 1], (8, 128))

        cols = [{k: column(u, k) for k in range(s, 4)} for u in range(8)]
        cell = {(i, j): spread(cols[j][s], i) for j in range(8) for i in range(j + 1)}
        invs, lines, sides = [], [], []
        for t in range(8):
            inv = lax.rsqrt(cell[t, t])
            invs.append(inv)
            for j in range(t + 1, 8):
                cell[t, j] = cell[t, j] * inv
            for i in range(t + 1, 8):
                for j in range(i, 8):
                    cell[i, j] = cell[i, j] - cell[t, i] * cell[t, j]
            line = [spread(x, t) for x in tiles[s]]
            side = {k: cols[t][k] for k in range(s + 1, 4)}
            for v in range(t):
                line = [x - cell[v, t] * y for x, y in zip(line, lines[v])]
                side = {k: x - cell[v, t] * sides[v][k] for k, x in side.items()}
            lines.append([x * inv for x in line])
            sides.append({k: x * inv for k, x in side.items()})
        for l in range(lanes):
            done = lines[0][l]
            for t in range(1, 8):
                done = jnp.where(spot == t, lines[t][l], done)
            out[pl.ds(base + 8 * s, 8), 128 * l:128 * l + 128] = done
        for k in range(s + 1, 4):
            for t in range(8):
                for l in range(lanes + 1):
                    tiles[k][l] = tiles[k][l] - sides[t][k] * lines[t][l]


def tn(a, b):
    return lax.dot_general(
        a, b, (((0,), (0,)), ((), ())), precision=lax.Precision.HIGHEST, preferred_element_type=F32
    )


def finish_kernel(nw, gd, gc, lead, core_in, out, core_out, g01, work, tail, sem):
    move = pltpu.make_async_copy(core_in, core_out, sem)
    move.start()
    rpp = 128 // nw
    for k in range(4):
        for j in range(nw):
            row = 128 * (k % 2) + rpp * j
            lane = 128 * (k // 2)
            g01[row:row + rpp, lane:lane + 128] = gc[k, j]
            if k >= 2:
                for l in range(k % 2, 2):
                    work[row:row + rpp, 128 * l:128 * l + 128] = gd[k, j, l]
    work[128:, :128] = jnp.zeros((128, 128), F32)
    row = lax.broadcasted_iota(jnp.int32, (256, 256), 0)
    col = lax.broadcasted_iota(jnp.int32, (256, 256), 1)
    upper = col >= row
    out[:256, :256] = jnp.where(upper, lead[:, :256], 0.0)
    out[256:, :256] = jnp.zeros((256, 256), F32)
    side = lax.dot_general(
        lead[:, 256:], g01[...], (((1,), (0,)), ((), ())),
        precision=lax.Precision.HIGHEST, preferred_element_type=F32,
    )
    out[:256, 256:] = side
    work[...] -= tn(side, side)
    for b in range(2):
        top = 128 * b
        for g in range(4):
            base = top + 32 * g
            eliminate(work, tail, base, top, 32 * g)
            if g < 3:
                work[base + 32:top + 128, top:] -= tn(
                    tail[base:base + 32, base + 32:top + 128], tail[base:base + 32, top:]
                )
        if b == 0:
            work[128:, 128:] -= tn(tail[:128, 128:], tail[:128, 128:])
    out[256:, 256:] = jnp.where(upper, tail[...], 0.0)
    move.wait()


def finish(nw, gd, gc, lead, core):
    vmem = pl.BlockSpec(memory_space=pltpu.VMEM)
    anywhere = pl.BlockSpec(memory_space=pl.ANY)
    return pl.pallas_call(
        functools.partial(finish_kernel, nw),
        out_shape=(
            jax.ShapeDtypeStruct((512, 512), F32),
            jax.ShapeDtypeStruct(core.shape, F32),
        ),
        in_specs=[vmem, vmem, vmem, anywhere],
        out_specs=(vmem, anywhere),
        scratch_shapes=[
            pltpu.VMEM((256, 256), F32),
            pltpu.VMEM((256, 256), F32),
            pltpu.VMEM((256, 256), F32),
            pltpu.SemaphoreType.DMA,
        ],
        compiler_params=pltpu.CompilerParams(vmem_limit_bytes=32 * 1024 * 1024),
    )(gd, gc, lead, core)


def on_device(nw, slab, factor):
    ncol = slab.shape[0] * slab.shape[2] * nw * slab.shape[3]
    return finish(nw, *exchange(nw, ncol, slab, factor.T))


def solution(mesh):
    return jax.shard_map(
        functools.partial(on_device, mesh.shape["wide"]),
        mesh=mesh,
        in_specs=(P(None, "narrow", "wide", None), P()),
        out_specs=(P(), P(None, None, "wide", "narrow")),
        check_vma=False,
    )
```

```python
import functools
import jax
import jax.numpy as jnp
from jax import lax
from jax.experimental import pallas as pl
from jax.experimental.pallas import tpu as pltpu
from jax.sharding import PartitionSpec as P

MESH = pl.DeviceIdType.MESH
F32 = jnp.float32
BF16 = jnp.bfloat16


def split(x):
    hi = x.astype(BF16)
    return hi, (x - hi.astype(F32)).astype(BF16)


def nt(a, b):
    return lax.dot_general(a, b, (((1,), (1,)), ((), ())), preferred_element_type=F32)


def nn(a, b):
    return lax.dot_general(a, b, (((1,), (0,)), ((), ())), preferred_element_type=F32)


def exchange_kernel(
    nw, scale, slab, ft, gd, gc, lead, core,
    mine, far, own_h, own_l, far_h, far_l, fac, diag1, diag2, cross,
    half, half_in, dpiece, dpiece_in, quarter, quarter_in, cpiece, cpiece_in,
    core_keep, core_give, work,
    far_send, far_recv, sib_send, sib_recv, loc_sem,
    half_sems, dw_send, dw_recv, da_send, da_recv, dn_send, dn_recv,
    q_send, q_recv, cw_send, cw_recv, ca_send, ca_recv, cn_send, cn_recv,
    core_sems, keep_sem,
):
    w = lax.axis_index("wide")
    n = lax.axis_index("narrow")
    p, q = n // 2, n % 2
    o, z = 1 - p, 1 - q
    sib = 2 * p + z
    ncomp = slab.shape[0]
    rows = slab.shape[1]

    barrier = pltpu.get_barrier_semaphore()
    for d in range(1, 4):
        pl.semaphore_signal(barrier, inc=1, device_id={"narrow": (n + d) % 4}, device_id_type=MESH)

    @pl.loop(1, nw)
    def _(d):
        pl.semaphore_signal(barrier, inc=1, device_id={"wide": (w + d) % nw}, device_id_type=MESH)

    pl.semaphore_wait(barrier, 3 + nw - 1)

    def remote(src, dst, ssem, rsem, **where):
        return pltpu.make_async_remote_copy(
            src_ref=src, dst_ref=dst, send_sem=ssem, recv_sem=rsem,
            device_id=where, device_id_type=MESH,
        )

    def lane_half(h):
        return pl.ds(pl.multiple_of(h * 128, 128), 128)

    def row_tile(t):
        return pl.ds(pl.multiple_of(t * 8, 8), 8)

    def far_copy(c, m):
        return remote(
            slab.at[c, :, pl.ds(8 * m, 8), lane_half(o)], far.at[q, c],
            far_send.at[c, m], far_recv.at[c, q], narrow=2 * o + m,
        )

    def sib_copy(c, l):
        return remote(
            slab.at[c, :, row_tile(z), pl.ds(128 * l, 128)], mine.at[q, c, l],
            sib_send.at[c, l], sib_recv.at[c, l], narrow=sib,
        )

    def loc_copy(c, l):
        return pltpu.make_async_copy(
            slab.at[c, :, row_tile(q), pl.ds(128 * l, 128)], mine.at[q, c, l], loc_sem.at[c, l]
        )

    last = ncomp - 1
    early = ncomp // 2

    def far_start(first, stop):
        for c in range(first, stop):
            far_copy(c, 0).start()
            far_copy(c, 1).start()

    far_start(0, 1)
    for c in range(ncomp):
        for l in range(2):
            sib_copy(c, l).start()
            loc_copy(c, l).start()
    far_start(1, early)

    for h in range(2):
        hi, lo = split(ft[:, 256 * h:256 * h + 256])
        fac[h, :64, :] = hi
        fac[h, 64:, :] = lo
    diag1[...] = jnp.zeros_like(diag1)
    diag2[...] = jnp.zeros_like(diag2)
    cross[...] = jnp.zeros_like(cross)

    mine_rows = mine.reshape(2, ncomp, 2, rows * 8, 128)
    far_rows = far.reshape(2, ncomp, rows * 8, 128)

    @pl.loop(0, ncomp)
    def _(c):
        for l in range(2):
            loc_copy(c, l).wait()
            remote(
                mine.at[z, c, l], mine.at[z, c, l], sib_send.at[c, l], sib_recv.at[c, l], narrow=sib
            ).wait_recv()
        for l in range(2):
            for m in range(2):
                for a in range(8):
                    hi, lo = split(mine_rows[m, c, l, pl.ds(a, rows, stride=8), :])
                    own_h[c, l, rows * m:rows * m + rows, 128 * a:128 * a + 128] = hi
                    own_l[c, l, rows * m:rows * m + rows, 128 * a:128 * a + 128] = lo
            diag1[...] += nt(own_h[c, l], own_h[c, l])
            diag2[...] += nt(own_h[c, l], own_l[c, l])

    def scatter_sum(pieces, pieces_in, ssem, rsem):
        def copy(j):
            return remote(pieces.at[j], pieces_in.at[w], ssem.at[j], rsem.at[w], wide=j)

        @pl.loop(1, nw)
        def _(d):
            copy((w + d) % nw).start()

        pieces_in[w] = pieces[w]

        @pl.loop(1, nw)
        def _(d):
            j = (w + d) % nw
            remote(pieces.at[j], pieces_in.at[j], ssem.at[j], rsem.at[j], wide=j).wait_recv()

        total = pieces_in[0]
        for j in range(1, nw):
            total = total + pieces_in[j]
        return total

    def gather_all(full, ssem, rsem):
        def copy(j, slot):
            return remote(full.at[n, slot], full.at[n, slot], ssem.at[j], rsem.at[slot], wide=j)

        @pl.loop(1, nw)
        def _(d):
            copy((w + d) % nw, w).start()

        @pl.loop(1, nw)
        def _(d):
            j = (w + d) % nw
            copy(j, j).wait_recv()

    def share_copy(i, slot, k, then):
        def part(l):
            block = gd.at[slot, :, l]
            return remote(block, block, dn_send.at[i, l], dn_recv.at[slot, l], narrow=k)

        then(part(1))

        @pl.when(slot % 2 == 0)
        def _():
            then(part(0))

    def start(copy):
        copy.start()

    def arrived(copy):
        copy.wait_recv()

    def sent(copy):
        copy.wait_send()

    def cross_share(i, slot, k):
        return remote(gc.at[slot], gc.at[slot], cn_send.at[i], cn_recv.at[slot], narrow=k)

    rpp = 128 // nw

    mixed = diag2[...]
    whole = diag1[...] + (mixed + mixed.T)
    half[0] = whole[:128]
    half[1] = whole[128:]
    swap = remote(half.at[z], half_in, half_sems.at[0], half_sems.at[1], narrow=sib)
    swap.start()
    swap.wait()
    part = half[q] + half_in[...]
    for j in range(nw):
        for l in range(2):
            dpiece[j, l] = part[rpp * j:rpp * j + rpp, 128 * l:128 * l + 128]
    gd[n, w] = scatter_sum(dpiece, dpiece_in, dw_send, dw_recv) * scale
    gather_all(gd, da_send, da_recv)
    far_same = 2 * o + q
    far_cross = 2 * o + z
    share_copy(1, n, far_same, start)
    share_copy(0, n, sib, start)
    far_start(early, ncomp)

    def add_cross(c):
        for m in range(2):
            remote(
                far.at[m, c], far.at[m, c], far_send.at[c, m], far_recv.at[c, m], narrow=2 * o + m
            ).wait_recv()
            here = slice(rows * m, rows * m + rows)
            for a in range(8):
                hi, lo = split(far_rows[m, c, pl.ds(a, rows, stride=8), :])
                far_h[here, 128 * a:128 * a + 128] = hi
                far_l[here, 128 * a:128 * a + 128] = lo

            @pl.when(p == 0)
            def _():
                cross[:, here] += nt(own_h[c, 0], far_h[here, :]) + (
                    nt(own_h[c, 0], far_l[here, :]) + nt(own_l[c, 0], far_h[here, :])
                )

            @pl.when(p == 1)
            def _():
                cross[here, :] += nt(far_h[here, :], own_h[c, 1]) + (
                    nt(far_l[here, :], own_h[c, 1]) + nt(far_h[here, :], own_l[c, 1])
                )


    def keep_copy(c):
        return pltpu.make_async_copy(core_keep.at[c], core.at[c, :, row_tile(q), :], keep_sem.at[c])

    def give_copy(c, t):
        return remote(
            core_give.at[c], core.at[c, :, row_tile(t), :], core_sems.at[0, c], core_sems.at[1, c], narrow=sib
        )

    def make_core(c):
        both = nn(fac[p], own_h[c, p]) + nn(fac[o], far_h[...])
        low = nn(fac[p, :64], own_l[c, p]) + nn(fac[o, :64], far_l[...])
        value = both[:64] + (both[64:] + low)
        keep_rows = core_keep.at[c].reshape(64 * 8, 64)
        give_rows = core_give.at[c].reshape(64 * 8, 64)
        for a in range(8):
            left = value[:, 128 * a:128 * a + 64]
            right = value[:, 128 * a + 64:128 * a + 128]
            keep_rows[pl.ds(a, 64, stride=8), :] = jnp.where(q == 0, left, right)
            give_rows[pl.ds(a, 64, stride=8), :] = jnp.where(q == 0, right, left)
        keep_copy(c).start()
        give_copy(c, q).start()

    @pl.loop(0, early)
    def _(c):
        add_cross(c)
        make_core(c)

    share_copy(0, sib, sib, arrived)
    share_copy(1, far_same, far_same, arrived)
    share_copy(2, far_same, sib, start)
    share_copy(2, far_cross, sib, arrived)

    for k in range(2):
        for j in range(nw):
            for l in range(k, 2):
                work[128 * k + rpp * j:128 * k + rpp * j + rpp, 128 * l:128 * l + 128] = gd[k, j, l]
    work[128:, :128] = jnp.zeros((128, 128), F32)
    row = lax.broadcasted_iota(jnp.int32, (256, 256), 0)
    col = lax.broadcasted_iota(jnp.int32, (256, 256), 1)
    work[:, 256:] = (row == col).astype(F32)

    @pl.loop(0, 2)
    def _(b):
        top = pl.multiple_of(b * 128, 128)
        for g in range(4):
            base = pl.multiple_of(b * 128 + 32 * g, 32)
            eliminate(work, lead, base, 32 * g, 0, top)
            if g < 3:
                work[pl.ds(top, 128), :] -= tn(
                    lead[pl.ds(base, 32), pl.ds(top, 128)], lead[pl.ds(base, 32), :]
                )

        @pl.when(b == 0)
        def _():
            work[128:, :] -= tn(lead[:128, 128:256], lead[:128, :])

    @pl.loop(early, last)
    def _(c):
        add_cross(c)
        make_core(c)

    add_cross(last)
    block = cross[...]
    for k in range(4):
        l, h = k // 2, k % 2
        quarter[k] = block[128 * h:128 * h + 128, 128 * l:128 * l + 128]

    def quarter_copy(k, slot):
        return remote(quarter.at[k], quarter_in.at[slot], q_send.at[k], q_recv.at[slot], narrow=k)

    for d in range(1, 4):
        quarter_copy((n + d) % 4, n).start()
    make_core(last)
    quarter_in[n] = quarter[n]
    for d in range(1, 4):
        quarter_copy((n + d) % 4, (n + d) % 4).wait_recv()
    part = (quarter_in[0] + quarter_in[1]) + (quarter_in[2] + quarter_in[3])
    for j in range(nw):
        cpiece[j] = part[rpp * j:rpp * j + rpp]
    gc[n, w] = scatter_sum(cpiece, cpiece_in, cw_send, cw_recv) * scale
    gather_all(gc, ca_send, ca_recv)
    for d in range(1, 4):
        k = (n + d) % 4
        cross_share(d, n, k).start()
    for d in range(1, 4):
        k = (n + d) % 4
        cross_share(d, k, k).wait_recv()
    for d in range(1, 4):
        quarter_copy((n + d) % 4, n).wait_send()
        cross_share(d, n, (n + d) % 4).wait_send()

    @pl.loop(1, nw)
    def _(d):
        j = (w + d) % nw
        remote(dpiece.at[j], dpiece_in.at[w], dw_send.at[j], dw_recv.at[w], wide=j).wait_send()
        remote(gd.at[n, w], gd.at[n, w], da_send.at[j], da_recv.at[w], wide=j).wait_send()
        remote(cpiece.at[j], cpiece_in.at[w], cw_send.at[j], cw_recv.at[w], wide=j).wait_send()
        remote(gc.at[n, w], gc.at[n, w], ca_send.at[j], ca_recv.at[w], wide=j).wait_send()

    share_copy(0, n, sib, sent)
    share_copy(1, n, far_same, sent)
    share_copy(2, far_same, sib, sent)

    for c in range(ncomp):
        for m in range(2):
            far_copy(c, m).wait_send()
        for l in range(2):
            sib_copy(c, l).wait_send()
        keep_copy(c).wait()
        give_copy(c, q).wait_send()
        give_copy(c, z).wait_recv()


def exchange(nw, ncol, slab, ft):
    ncomp, rows, _, _ = slab.shape
    rank = ft.shape[0]
    rpp = 128 // nw
    dma = pltpu.SemaphoreType.DMA
    vmem = pl.BlockSpec(memory_space=pltpu.VMEM)
    anywhere = pl.BlockSpec(memory_space=pl.ANY)
    return pl.pallas_call(
        functools.partial(exchange_kernel, nw, 1.0 / ncol),
        out_shape=(
            jax.ShapeDtypeStruct((4, nw, 2, rpp, 128), F32),
            jax.ShapeDtypeStruct((4, nw, rpp, 128), F32),
            jax.ShapeDtypeStruct((256, 512), F32),
            jax.ShapeDtypeStruct((ncomp, rank, 16, 64), F32),
        ),
        in_specs=[anywhere, vmem],
        out_specs=(vmem, vmem, vmem, anywhere),
        scratch_shapes=[
            pltpu.VMEM((2, ncomp, 2, rows, 8, 128), F32),
            pltpu.VMEM((2, ncomp, rows, 8, 128), F32),
            pltpu.VMEM((ncomp, 2, 256, 1024), BF16),
            pltpu.VMEM((ncomp, 2, 256, 1024), BF16),
            pltpu.VMEM((256, 1024), BF16),
            pltpu.VMEM((256, 1024), BF16),
            pltpu.VMEM((2, 128, 256), BF16),
            pltpu.VMEM((256, 256), F32),
            pltpu.VMEM((256, 256), F32),
            pltpu.VMEM((256, 256), F32),
            pltpu.VMEM((2, 128, 256), F32),
            pltpu.VMEM((128, 256), F32),
            pltpu.VMEM((nw, 2, rpp, 128), F32),
            pltpu.VMEM((nw, 2, rpp, 128), F32),
            pltpu.VMEM((4, 128, 128), F32),
            pltpu.VMEM((4, 128, 128), F32),
            pltpu.VMEM((nw, rpp, 128), F32),
            pltpu.VMEM((nw, rpp, 128), F32),
            pltpu.VMEM((ncomp, rank, 8, 64), F32),
            pltpu.VMEM((ncomp, rank, 8, 64), F32),
            pltpu.VMEM((256, 512), F32),
            dma((ncomp, 2)), dma((ncomp, 2)), dma((ncomp, 2)), dma((ncomp, 2)), dma((ncomp, 2)),
            dma((2,)), dma((nw,)), dma((nw,)), dma((nw,)), dma((nw,)), dma((3, 2)), dma((4, 2)),
            dma((4,)), dma((4,)), dma((nw,)), dma((nw,)), dma((nw,)), dma((nw,)), dma((4,)), dma((4,)),
            dma((2, ncomp)), dma((ncomp,)),
        ],
        compiler_params=pltpu.CompilerParams(
            collective_id=0, has_side_effects=True, vmem_limit_bytes=48 * 1024 * 1024
        ),
    )(slab, ft)


def eliminate(work, out, base, offset, first, top=None):
    start = 128 * first
    lanes = work.shape[1] // 128 - first
    spot = lax.broadcasted_iota(jnp.int32, (8, 128), 0)

    def spread(x, t):
        return jnp.broadcast_to(x[t:t + 1, :], (8, 128))

    rows = [work[pl.ds(base + 8 * s, 8), start:] for s in range(4)]
    tiles = [[r[:, 128 * l:128 * l + 128] for l in range(lanes)] for r in rows]
    lead = 0
    if top is not None:
        lead = lanes
        for s in range(4):
            tiles[s].append(work[pl.ds(base + 8 * s, 8), pl.ds(top, 128)])
    for s in range(4):
        def column(u, k):
            at = offset + 8 * s + u
            return jnp.broadcast_to(tiles[k][lead][:, at:at + 1], (8, 128))

        cols = [{k: column(u, k) for k in range(s, 4)} for u in range(8)]
        cell = {(i, j): spread(cols[j][s], i) for j in range(8) for i in range(j + 1)}
        invs, lines, sides = [], [], []
        for t in range(8):
            inv = lax.rsqrt(cell[t, t])
            invs.append(inv)
            for j in range(t + 1, 8):
                cell[t, j] = cell[t, j] * inv
            for i in range(t + 1, 8):
                for j in range(i, 8):
                    cell[i, j] = cell[i, j] - cell[t, i] * cell[t, j]
            line = [spread(x, t) for x in tiles[s]]
            side = {k: cols[t][k] for k in range(s + 1, 4)}
            for v in range(t):
                line = [x - cell[v, t] * y for x, y in zip(line, lines[v])]
                side = {k: x - cell[v, t] * sides[v][k] for k, x in side.items()}
            lines.append([x * inv for x in line])
            sides.append({k: x * inv for k, x in side.items()})
        for l in range(lanes):
            done = lines[0][l]
            for t in range(1, 8):
                done = jnp.where(spot == t, lines[t][l], done)
            out[pl.ds(base + 8 * s, 8), start + 128 * l:start + 128 * l + 128] = done
        for k in range(s + 1, 4):
            for t in range(8):
                for l in range(len(tiles[k])):
                    tiles[k][l] = tiles[k][l] - sides[t][k] * lines[t][l]


def tn(a, b):
    return lax.dot_general(
        a, b, (((0,), (0,)), ((), ())), precision=lax.Precision.HIGHEST, preferred_element_type=F32
    )


def finish_kernel(nw, gd, gc, lead, core_in, out, core_out, g01, work, tail, sem):
    move = pltpu.make_async_copy(core_in, core_out, sem)
    move.start()
    rpp = 128 // nw
    for k in range(4):
        for j in range(nw):
            row = 128 * (k % 2) + rpp * j
            lane = 128 * (k // 2)
            g01[row:row + rpp, lane:lane + 128] = gc[k, j]
            if k >= 2:
                for l in range(k % 2, 2):
                    work[row:row + rpp, 128 * l:128 * l + 128] = gd[k, j, l]
    work[128:, :128] = jnp.zeros((128, 128), F32)
    row = lax.broadcasted_iota(jnp.int32, (256, 256), 0)
    col = lax.broadcasted_iota(jnp.int32, (256, 256), 1)
    upper = col >= row
    out[:256, :256] = jnp.where(upper, lead[:, :256], 0.0)
    out[256:, :256] = jnp.zeros((256, 256), F32)
    side = lax.dot_general(
        lead[:, 256:], g01[...], (((1,), (0,)), ((), ())),
        precision=lax.Precision.HIGHEST, preferred_element_type=F32,
    )
    out[:256, 256:] = side
    work[...] -= tn(side, side)
    for b in range(2):
        top = 128 * b
        for g in range(4):
            base = top + 32 * g
            eliminate(work, tail, base, 32 * g, b)
            if g < 3:
                work[base + 32:top + 128, top:] -= tn(
                    tail[base:base + 32, base + 32:top + 128], tail[base:base + 32, top:]
                )
        if b == 0:
            work[128:, 128:] -= tn(tail[:128, 128:], tail[:128, 128:])
    tail[128:, :128] = jnp.zeros((128, 128), F32)
    out[256:, 256:] = jnp.where(upper, tail[...], 0.0)
    move.wait()


def finish(nw, gd, gc, lead, core):
    vmem = pl.BlockSpec(memory_space=pltpu.VMEM)
    anywhere = pl.BlockSpec(memory_space=pl.ANY)
    return pl.pallas_call(
        functools.partial(finish_kernel, nw),
        out_shape=(
            jax.ShapeDtypeStruct((512, 512), F32),
            jax.ShapeDtypeStruct(core.shape, F32),
        ),
        in_specs=[vmem, vmem, vmem, anywhere],
        out_specs=(vmem, anywhere),
        scratch_shapes=[
            pltpu.VMEM((256, 256), F32),
            pltpu.VMEM((256, 256), F32),
            pltpu.VMEM((256, 256), F32),
            pltpu.SemaphoreType.DMA,
        ],
        compiler_params=pltpu.CompilerParams(vmem_limit_bytes=32 * 1024 * 1024),
    )(gd, gc, lead, core)


def on_device(nw, slab, factor):
    ncol = slab.shape[0] * slab.shape[2] * nw * slab.shape[3]
    return finish(nw, *exchange(nw, ncol, slab, factor.T))


def solution(mesh):
    return jax.shard_map(
        functools.partial(on_device, mesh.shape["wide"]),
        mesh=mesh,
        in_specs=(P(None, "narrow", "wide", None), P()),
        out_specs=(P(), P(None, None, "wide", "narrow")),
        check_vma=False,
    )
```

```python
import functools
import jax
import jax.numpy as jnp
from jax import lax
from jax.experimental import pallas as pl
from jax.experimental.pallas import tpu as pltpu
from jax.sharding import PartitionSpec as P

MESH = pl.DeviceIdType.MESH
F32 = jnp.float32
BF16 = jnp.bfloat16


def split(x):
    hi = x.astype(BF16)
    return hi, (x - hi.astype(F32)).astype(BF16)


def nt(a, b):
    return lax.dot_general(a, b, (((1,), (1,)), ((), ())), preferred_element_type=F32)


def nn(a, b):
    return lax.dot_general(a, b, (((1,), (0,)), ((), ())), preferred_element_type=F32)


def exchange_kernel(
    nw, scale, slab, ft, gd, gc, lead, core,
    mine, far, own_h, own_l, far_h, far_l, fac, diag1, diag2, cross,
    half, half_in, dpiece, dpiece_in, quarter, quarter_in, cpiece, cpiece_in,
    core_keep, core_give, work,
    far_send, far_recv, sib_send, sib_recv, loc_sem,
    half_sems, dw_send, dw_recv, da_send, da_recv, dn_send, dn_recv,
    q_send, q_recv, cw_send, cw_recv, ca_send, ca_recv, cn_send, cn_recv,
    core_sems, keep_sem,
):
    w = lax.axis_index("wide")
    n = lax.axis_index("narrow")
    p, q = n // 2, n % 2
    o, z = 1 - p, 1 - q
    sib = 2 * p + z
    ncomp = slab.shape[0]
    rows = slab.shape[1]

    barrier = pltpu.get_barrier_semaphore()
    for d in range(1, 4):
        pl.semaphore_signal(barrier, inc=1, device_id={"narrow": (n + d) % 4}, device_id_type=MESH)

    @pl.loop(1, nw)
    def _(d):
        pl.semaphore_signal(barrier, inc=1, device_id={"wide": (w + d) % nw}, device_id_type=MESH)

    pl.semaphore_wait(barrier, 3 + nw - 1)

    def remote(src, dst, ssem, rsem, **where):
        return pltpu.make_async_remote_copy(
            src_ref=src, dst_ref=dst, send_sem=ssem, recv_sem=rsem,
            device_id=where, device_id_type=MESH,
        )

    def lane_half(h):
        return pl.ds(pl.multiple_of(h * 128, 128), 128)

    def row_tile(t):
        return pl.ds(pl.multiple_of(t * 8, 8), 8)

    def far_copy(c, m):
        return remote(
            slab.at[c, :, pl.ds(8 * m, 8), lane_half(o)], far.at[q, c],
            far_send.at[c, m], far_recv.at[c, q], narrow=2 * o + m,
        )

    def sib_copy(c, l):
        return remote(
            slab.at[c, :, row_tile(z), pl.ds(128 * l, 128)], mine.at[q, c, l],
            sib_send.at[c, l], sib_recv.at[c, l], narrow=sib,
        )

    def loc_copy(c, l):
        return pltpu.make_async_copy(
            slab.at[c, :, row_tile(q), pl.ds(128 * l, 128)], mine.at[q, c, l], loc_sem.at[c, l]
        )

    last = ncomp - 1
    early = ncomp // 2

    def far_start(first, stop):
        for c in range(first, stop):
            far_copy(c, 0).start()
            far_copy(c, 1).start()

    far_start(0, 1)
    for c in range(ncomp):
        for l in range(2):
            sib_copy(c, l).start()
            loc_copy(c, l).start()
    far_start(1, early)

    for h in range(2):
        hi, lo = split(ft[:, 256 * h:256 * h + 256])
        fac[h, :64, :] = hi
        fac[h, 64:, :] = lo
    diag1[...] = jnp.zeros_like(diag1)
    diag2[...] = jnp.zeros_like(diag2)
    cross[...] = jnp.zeros_like(cross)

    mine_rows = mine.reshape(2, ncomp, 2, rows * 8, 128)
    far_rows = far.reshape(2, ncomp, rows * 8, 128)

    @pl.loop(0, ncomp)
    def _(c):
        for l in range(2):
            loc_copy(c, l).wait()
            remote(
                mine.at[z, c, l], mine.at[z, c, l], sib_send.at[c, l], sib_recv.at[c, l], narrow=sib
            ).wait_recv()
        for l in range(2):
            for m in range(2):
                for a in range(8):
                    hi, lo = split(mine_rows[m, c, l, pl.ds(a, rows, stride=8), :])
                    own_h[c, l, rows * m:rows * m + rows, 128 * a:128 * a + 128] = hi
                    own_l[c, l, rows * m:rows * m + rows, 128 * a:128 * a + 128] = lo
            diag1[...] += nt(own_h[c, l], own_h[c, l])
            diag2[...] += nt(own_h[c, l], own_l[c, l])

    def scatter_sum(pieces, pieces_in, ssem, rsem):
        def copy(j):
            return remote(pieces.at[j], pieces_in.at[w], ssem.at[j], rsem.at[w], wide=j)

        @pl.loop(1, nw)
        def _(d):
            copy((w + d) % nw).start()

        pieces_in[w] = pieces[w]

        @pl.loop(1, nw)
        def _(d):
            j = (w + d) % nw
            remote(pieces.at[j], pieces_in.at[j], ssem.at[j], rsem.at[j], wide=j).wait_recv()

        total = pieces_in[0]
        for j in range(1, nw):
            total = total + pieces_in[j]
        return total

    def gather_all(full, ssem, rsem):
        def copy(j, slot):
            return remote(full.at[n, slot], full.at[n, slot], ssem.at[j], rsem.at[slot], wide=j)

        @pl.loop(1, nw)
        def _(d):
            copy((w + d) % nw, w).start()

        @pl.loop(1, nw)
        def _(d):
            j = (w + d) % nw
            copy(j, j).wait_recv()

    def share_copy(i, slot, k, then):
        def part(l):
            block = gd.at[slot, :, l]
            return remote(block, block, dn_send.at[i, l], dn_recv.at[slot, l], narrow=k)

        then(part(1))

        @pl.when(slot % 2 == 0)
        def _():
            then(part(0))

    def start(copy):
        copy.start()

    def arrived(copy):
        copy.wait_recv()

    def sent(copy):
        copy.wait_send()

    def cross_share(i, slot, k):
        return remote(gc.at[slot], gc.at[slot], cn_send.at[i], cn_recv.at[slot], narrow=k)

    rpp = 128 // nw

    mixed = diag2[...]
    whole = diag1[...] + (mixed + mixed.T)
    half[0] = whole[:128]
    half[1] = whole[128:]
    swap = remote(half.at[z], half_in, half_sems.at[0], half_sems.at[1], narrow=sib)
    swap.start()
    swap.wait()
    part = half[q] + half_in[...]
    for j in range(nw):
        for l in range(2):
            dpiece[j, l] = part[rpp * j:rpp * j + rpp, 128 * l:128 * l + 128]
    gd[n, w] = scatter_sum(dpiece, dpiece_in, dw_send, dw_recv) * scale
    gather_all(gd, da_send, da_recv)
    far_same = 2 * o + q
    far_cross = 2 * o + z
    share_copy(1, n, far_same, start)
    share_copy(0, n, sib, start)
    far_start(early, ncomp)

    def add_cross(c):
        for m in range(2):
            remote(
                far.at[m, c], far.at[m, c], far_send.at[c, m], far_recv.at[c, m], narrow=2 * o + m
            ).wait_recv()
            here = slice(rows * m, rows * m + rows)
            for a in range(8):
                hi, lo = split(far_rows[m, c, pl.ds(a, rows, stride=8), :])
                far_h[here, 128 * a:128 * a + 128] = hi
                far_l[here, 128 * a:128 * a + 128] = lo

            @pl.when(p == 0)
            def _():
                cross[:, here] += nt(own_h[c, 0], far_h[here, :]) + (
                    nt(own_h[c, 0], far_l[here, :]) + nt(own_l[c, 0], far_h[here, :])
                )

            @pl.when(p == 1)
            def _():
                cross[here, :] += nt(far_h[here, :], own_h[c, 1]) + (
                    nt(far_l[here, :], own_h[c, 1]) + nt(far_h[here, :], own_l[c, 1])
                )


    def keep_copy(c):
        return pltpu.make_async_copy(core_keep.at[c], core.at[c, :, row_tile(q), :], keep_sem.at[c])

    def give_copy(c, t):
        return remote(
            core_give.at[c], core.at[c, :, row_tile(t), :], core_sems.at[0, c], core_sems.at[1, c], narrow=sib
        )

    def make_core(c):
        both = nn(fac[p], own_h[c, p]) + nn(fac[o], far_h[...])
        low = nn(fac[p, :64], own_l[c, p]) + nn(fac[o, :64], far_l[...])
        value = both[:64] + (both[64:] + low)
        keep_rows = core_keep.at[c].reshape(64 * 8, 64)
        give_rows = core_give.at[c].reshape(64 * 8, 64)
        for a in range(8):
            left = value[:, 128 * a:128 * a + 64]
            right = value[:, 128 * a + 64:128 * a + 128]
            keep_rows[pl.ds(a, 64, stride=8), :] = jnp.where(q == 0, left, right)
            give_rows[pl.ds(a, 64, stride=8), :] = jnp.where(q == 0, right, left)
        keep_copy(c).start()
        give_copy(c, q).start()

    @pl.loop(0, early)
    def _(c):
        add_cross(c)
        make_core(c)

    share_copy(0, sib, sib, arrived)
    share_copy(1, far_same, far_same, arrived)
    share_copy(2, far_same, sib, start)
    share_copy(2, far_cross, sib, arrived)

    for k in range(2):
        for j in range(nw):
            for l in range(k, 2):
                work[128 * k + rpp * j:128 * k + rpp * j + rpp, 128 * l:128 * l + 128] = gd[k, j, l]
    work[128:, :128] = jnp.zeros((128, 128), F32)
    row = lax.broadcasted_iota(jnp.int32, (256, 256), 0)
    col = lax.broadcasted_iota(jnp.int32, (256, 256), 1)
    work[:, 256:] = (row == col).astype(F32)

    @pl.loop(0, 2)
    def _(b):
        top = pl.multiple_of(b * 128, 128)
        for g in range(4):
            base = pl.multiple_of(b * 128 + 32 * g, 32)
            eliminate(work, lead, base, 32, 32 * g, 0, top)
            if g < 3:
                work[pl.ds(top, 128), :] -= tn(
                    lead[pl.ds(base, 32), pl.ds(top, 128)], lead[pl.ds(base, 32), :]
                )

        @pl.when(b == 0)
        def _():
            work[128:, :] -= tn(lead[:128, 128:256], lead[:128, :])

    @pl.loop(early, last)
    def _(c):
        add_cross(c)
        make_core(c)

    add_cross(last)
    block = cross[...]
    for k in range(4):
        l, h = k // 2, k % 2
        quarter[k] = block[128 * h:128 * h + 128, 128 * l:128 * l + 128]

    def quarter_copy(k, slot):
        return remote(quarter.at[k], quarter_in.at[slot], q_send.at[k], q_recv.at[slot], narrow=k)

    for d in range(1, 4):
        quarter_copy((n + d) % 4, n).start()
    make_core(last)
    quarter_in[n] = quarter[n]
    for d in range(1, 4):
        quarter_copy((n + d) % 4, (n + d) % 4).wait_recv()
    part = (quarter_in[0] + quarter_in[1]) + (quarter_in[2] + quarter_in[3])
    for j in range(nw):
        cpiece[j] = part[rpp * j:rpp * j + rpp]
    gc[n, w] = scatter_sum(cpiece, cpiece_in, cw_send, cw_recv) * scale
    gather_all(gc, ca_send, ca_recv)
    for d in range(1, 4):
        k = (n + d) % 4
        cross_share(d, n, k).start()
    for d in range(1, 4):
        k = (n + d) % 4
        cross_share(d, k, k).wait_recv()
    for d in range(1, 4):
        quarter_copy((n + d) % 4, n).wait_send()
        cross_share(d, n, (n + d) % 4).wait_send()

    @pl.loop(1, nw)
    def _(d):
        j = (w + d) % nw
        remote(dpiece.at[j], dpiece_in.at[w], dw_send.at[j], dw_recv.at[w], wide=j).wait_send()
        remote(gd.at[n, w], gd.at[n, w], da_send.at[j], da_recv.at[w], wide=j).wait_send()
        remote(cpiece.at[j], cpiece_in.at[w], cw_send.at[j], cw_recv.at[w], wide=j).wait_send()
        remote(gc.at[n, w], gc.at[n, w], ca_send.at[j], ca_recv.at[w], wide=j).wait_send()

    share_copy(0, n, sib, sent)
    share_copy(1, n, far_same, sent)
    share_copy(2, far_same, sib, sent)

    for c in range(ncomp):
        for m in range(2):
            far_copy(c, m).wait_send()
        for l in range(2):
            sib_copy(c, l).wait_send()
        keep_copy(c).wait()
        give_copy(c, q).wait_send()
        give_copy(c, z).wait_recv()


def exchange(nw, ncol, slab, ft):
    ncomp, rows, _, _ = slab.shape
    rank = ft.shape[0]
    rpp = 128 // nw
    dma = pltpu.SemaphoreType.DMA
    vmem = pl.BlockSpec(memory_space=pltpu.VMEM)
    anywhere = pl.BlockSpec(memory_space=pl.ANY)
    return pl.pallas_call(
        functools.partial(exchange_kernel, nw, 1.0 / ncol),
        out_shape=(
            jax.ShapeDtypeStruct((4, nw, 2, rpp, 128), F32),
            jax.ShapeDtypeStruct((4, nw, rpp, 128), F32),
            jax.ShapeDtypeStruct((256, 512), F32),
            jax.ShapeDtypeStruct((ncomp, rank, 16, 64), F32),
        ),
        in_specs=[anywhere, vmem],
        out_specs=(vmem, vmem, vmem, anywhere),
        scratch_shapes=[
            pltpu.VMEM((2, ncomp, 2, rows, 8, 128), F32),
            pltpu.VMEM((2, ncomp, rows, 8, 128), F32),
            pltpu.VMEM((ncomp, 2, 256, 1024), BF16),
            pltpu.VMEM((ncomp, 2, 256, 1024), BF16),
            pltpu.VMEM((256, 1024), BF16),
            pltpu.VMEM((256, 1024), BF16),
            pltpu.VMEM((2, 128, 256), BF16),
            pltpu.VMEM((256, 256), F32),
            pltpu.VMEM((256, 256), F32),
            pltpu.VMEM((256, 256), F32),
            pltpu.VMEM((2, 128, 256), F32),
            pltpu.VMEM((128, 256), F32),
            pltpu.VMEM((nw, 2, rpp, 128), F32),
            pltpu.VMEM((nw, 2, rpp, 128), F32),
            pltpu.VMEM((4, 128, 128), F32),
            pltpu.VMEM((4, 128, 128), F32),
            pltpu.VMEM((nw, rpp, 128), F32),
            pltpu.VMEM((nw, rpp, 128), F32),
            pltpu.VMEM((ncomp, rank, 8, 64), F32),
            pltpu.VMEM((ncomp, rank, 8, 64), F32),
            pltpu.VMEM((256, 512), F32),
            dma((ncomp, 2)), dma((ncomp, 2)), dma((ncomp, 2)), dma((ncomp, 2)), dma((ncomp, 2)),
            dma((2,)), dma((nw,)), dma((nw,)), dma((nw,)), dma((nw,)), dma((3, 2)), dma((4, 2)),
            dma((4,)), dma((4,)), dma((nw,)), dma((nw,)), dma((nw,)), dma((nw,)), dma((4,)), dma((4,)),
            dma((2, ncomp)), dma((ncomp,)),
        ],
        compiler_params=pltpu.CompilerParams(
            collective_id=0, has_side_effects=True, vmem_limit_bytes=48 * 1024 * 1024
        ),
    )(slab, ft)


def eliminate(work, out, base, depth, offset, first, top=None):
    start = 128 * first
    steps = depth // 8
    lanes = work.shape[1] // 128 - first
    spot = lax.broadcasted_iota(jnp.int32, (8, 128), 0)

    def spread(x, t):
        return jnp.broadcast_to(x[t:t + 1, :], (8, 128))

    rows = [work[pl.ds(base + 8 * s, 8), start:] for s in range(steps)]
    tiles = [[r[:, 128 * l:128 * l + 128] for l in range(lanes)] for r in rows]
    lead = 0
    if top is not None:
        lead = lanes
        for s in range(steps):
            tiles[s].append(work[pl.ds(base + 8 * s, 8), pl.ds(top, 128)])
    for s in range(steps):
        def column(u, k):
            at = offset + 8 * s + u
            return jnp.broadcast_to(tiles[k][lead][:, at:at + 1], (8, 128))

        cols = [{k: column(u, k) for k in range(s, steps)} for u in range(8)]
        cell = {(i, j): spread(cols[j][s], i) for j in range(8) for i in range(j + 1)}
        invs, lines, sides = [], [], []
        for t in range(8):
            inv = lax.rsqrt(cell[t, t])
            invs.append(inv)
            for j in range(t + 1, 8):
                cell[t, j] = cell[t, j] * inv
            for i in range(t + 1, 8):
                for j in range(i, 8):
                    cell[i, j] = cell[i, j] - cell[t, i] * cell[t, j]
            line = [spread(x, t) for x in tiles[s]]
            side = {k: cols[t][k] for k in range(s + 1, steps)}
            for v in range(t):
                line = [x - cell[v, t] * y for x, y in zip(line, lines[v])]
                side = {k: x - cell[v, t] * sides[v][k] for k, x in side.items()}
            lines.append([x * inv for x in line])
            sides.append({k: x * inv for k, x in side.items()})
        for l in range(lanes):
            done = lines[0][l]
            for t in range(1, 8):
                done = jnp.where(spot == t, lines[t][l], done)
            out[pl.ds(base + 8 * s, 8), start + 128 * l:start + 128 * l + 128] = done
        for k in range(s + 1, steps):
            for t in range(8):
                for l in range(len(tiles[k])):
                    tiles[k][l] = tiles[k][l] - sides[t][k] * lines[t][l]


def tn(a, b):
    return lax.dot_general(
        a, b, (((0,), (0,)), ((), ())), precision=lax.Precision.HIGHEST, preferred_element_type=F32
    )


def finish_kernel(nw, gd, gc, lead, core_in, out, core_out, g01, work, tail, sem):
    move = pltpu.make_async_copy(core_in, core_out, sem)
    move.start()
    rpp = 128 // nw
    for k in range(4):
        for j in range(nw):
            row = 128 * (k % 2) + rpp * j
            lane = 128 * (k // 2)
            g01[row:row + rpp, lane:lane + 128] = gc[k, j]
            if k >= 2:
                for l in range(k % 2, 2):
                    work[row:row + rpp, 128 * l:128 * l + 128] = gd[k, j, l]
    work[128:, :128] = jnp.zeros((128, 128), F32)
    row = lax.broadcasted_iota(jnp.int32, (256, 256), 0)
    col = lax.broadcasted_iota(jnp.int32, (256, 256), 1)
    upper = col >= row
    out[:256, :256] = jnp.where(upper, lead[:, :256], 0.0)
    out[256:, :256] = jnp.zeros((256, 256), F32)
    side = lax.dot_general(
        lead[:, 256:], g01[...], (((1,), (0,)), ((), ())),
        precision=lax.Precision.HIGHEST, preferred_element_type=F32,
    )
    out[:256, 256:] = side
    work[...] -= tn(side, side)
    for b in range(2):
        top = 128 * b
        middle = top + 64
        eliminate(work, tail, top, 64, 0, b)
        work[middle:top + 128, top:] -= tn(tail[top:middle, middle:top + 128], tail[top:middle, top:])
        eliminate(work, tail, middle, 64, 64, b)
        if b == 0:
            work[128:, 128:] -= tn(tail[:128, 128:], tail[:128, 128:])
    tail[128:, :128] = jnp.zeros((128, 128), F32)
    out[256:, 256:] = jnp.where(upper, tail[...], 0.0)
    move.wait()


def finish(nw, gd, gc, lead, core):
    vmem = pl.BlockSpec(memory_space=pltpu.VMEM)
    anywhere = pl.BlockSpec(memory_space=pl.ANY)
    return pl.pallas_call(
        functools.partial(finish_kernel, nw),
        out_shape=(
            jax.ShapeDtypeStruct((512, 512), F32),
            jax.ShapeDtypeStruct(core.shape, F32),
        ),
        in_specs=[vmem, vmem, vmem, anywhere],
        out_specs=(vmem, anywhere),
        scratch_shapes=[
            pltpu.VMEM((256, 256), F32),
            pltpu.VMEM((256, 256), F32),
            pltpu.VMEM((256, 256), F32),
            pltpu.SemaphoreType.DMA,
        ],
        compiler_params=pltpu.CompilerParams(vmem_limit_bytes=32 * 1024 * 1024),
    )(gd, gc, lead, core)


def on_device(nw, slab, factor):
    ncol = slab.shape[0] * slab.shape[2] * nw * slab.shape[3]
    return finish(nw, *exchange(nw, ncol, slab, factor.T))


def solution(mesh):
    return jax.shard_map(
        functools.partial(on_device, mesh.shape["wide"]),
        mesh=mesh,
        in_specs=(P(None, "narrow", "wide", None), P()),
        out_specs=(P(), P(None, None, "wide", "narrow")),
        check_vma=False,
    )
```
